32 devices in a mesh: groups: 2 (over x), dap: 8 (over z, y), rep: 2 (over core).
Axes of the slice: x: 2, y: 2, z: 4, core: 2. Of those that a mesh axis runs over, the one named last changes fastest.
Arguments:
- pair_input: bfloat16 [128, 64, 128], P(('groups', 'dap')), parts along dimension 0, may hold values from -6 to 6
- outgoing_weights: bfloat16 [4, 128, 128], P(None, None, 'rep'), may hold values from -0.5 to 0.5
- outgoing_gate: bfloat16 [128, 128], P(None, 'rep'), may hold values from -0.5 to 0.5
- outgoing_output: bfloat16 [128, 128], P('rep'), may hold values from -0.5 to 0.5
- incoming_weights: bfloat16 [4, 128, 128], P(None, None, 'rep'), may hold values from -0.5 to 0.5
- incoming_gate: bfloat16 [128, 128], P(None, 'rep'), may hold values from -0.5 to 0.5
- incoming_output: bfloat16 [128, 128], P('rep'), may hold values from -0.5 to 0.5
- distogram_head: bfloat16 [128, 64], replicated, may hold values from -0.5 to 0.5
- distance_bins: int32 [128, 64], P('groups'), parts along dimension 0, may hold values from 0 to 63
- chain_index: int32 [128], P('groups'), parts along dimension 0, may hold values from 0 to 7, as said below
- chain_swap: int32 [16], P('groups'), parts along dimension 0, may hold values from 0 to 7, as said below
Outputs:
- pair_grad: float32 [128, 64, 128], P(('groups', 'dap')), parts along dimension 0
- grad_outgoing_weights: float32 [8, 128, 128], P('groups', None, 'rep'), parts along dimension 0
- grad_outgoing_gate: float32 [256, 128], P('groups', 'rep'), parts along dimension 0
- grad_outgoing_output: float32 [256, 128], P(('groups', 'rep')), parts along dimension 0
- grad_incoming_weights: float32 [8, 128, 128], P('groups', None, 'rep'), parts along dimension 0
- grad_incoming_gate: float32 [256, 128], P('groups', 'rep'), parts along dimension 0
- grad_incoming_output: float32 [256, 128], P(('groups', 'rep')), parts along dimension 0
- grad_distogram_head: float32 [256, 64], P('groups'), parts along dimension 0
The draws below stay inside these ranges and needn't reach their ends.
There are 2 independent parts, one for each index of `groups`. The reference program is written for one: setup_inputs(seed, part) draws one part's arguments, and reference() takes and returns one part's arrays. A program takes and returns all parts, laid end to end along the dimension named above; an argument that names none is the same for every part. Nothing has to cross between parts.
Inputs may be any that keep to these rules, and one draw needn't show every extreme that they name: `chain_index`: never falls; every chain has at least one residue; chains 2m and 2m + 1 have equal lengths. `chain_swap`: A permutation of the chains that maps chain 2m to 2m or 2m + 1 and chain 2m + 1 to the other one.
All inputs are finite; a program needn't handle non-finite values.
Results may differ from the reference program's by a relative error of at most 0.025.
Values may be sent and summed in bfloat16 or wider, within the bound.
A program may use at most 192 MiB of HBM per device.

```python
import jax
import jax.numpy as jnp
from jax import lax

C = 128
H = 128
BINS = 64
NCH = 8
N = 64


def chain_layout(key):
    base_key = jax.random.fold_in(key, 11)
    half_count = N // 2
    pair_count = NCH // 2
    picked = jax.random.permutation(base_key, half_count - 1)[:pair_count - 1] + 1
    cut_points = jnp.sort(picked).astype(jnp.int32)
    bounds = jnp.concatenate([jnp.zeros((1,), jnp.int32), cut_points, jnp.full((1,), half_count, jnp.int32)])
    positions = jnp.arange(N, dtype=jnp.int32)
    which_pair = jnp.sum((positions[:, None] >= 2 * cut_points[None, :]).astype(jnp.int32), axis=1)
    pair_ids = jnp.arange(pair_count, dtype=jnp.int32)
    member = (which_pair[:, None] == pair_ids[None, :]).astype(jnp.int32)
    pair_start = jnp.sum(member * (2 * bounds[None, :-1]), axis=1)
    pair_length = jnp.sum(member * (bounds[None, 1:] - bounds[None, :-1]), axis=1)
    second_member = (positions - pair_start >= pair_length).astype(jnp.int32)
    chain_index = (2 * which_pair + second_member).astype(jnp.int32)
    swap_bits = jax.random.randint(jax.random.fold_in(key, 12), (pair_count,), 0, 2).astype(jnp.int32)
    even_chains = 2 * pair_ids
    chain_swap = jnp.stack([even_chains + swap_bits, even_chains + 1 - swap_bits], axis=1).reshape(-1)
    return (chain_index, chain_swap.astype(jnp.int32))


def draw_chain_index(key, part):
    return chain_layout(key)[0]


def draw_chain_swap(key, part):
    return chain_layout(key)[1]


def set_ends(drawn, stream_key, low, largest):
    spot = [jax.random.randint(jax.random.fold_in(stream_key, axis), (), 0, length) for axis, length in enumerate(drawn.shape)]
    main_axis = drawn.shape.index(max(drawn.shape))
    neighbour = spot[:main_axis] + [(spot[main_axis] + 1) % drawn.shape[main_axis]] + spot[main_axis + 1:]
    return drawn.at[tuple(spot)].set(low).at[tuple(neighbour)].set(largest)


def levels(key, extent, cuts, low, top_value):
    loudness = 1.0
    for dim, parts in cuts:
        steps = jax.random.uniform(jax.random.fold_in(jax.random.fold_in(key, 6), dim), (parts,), jnp.float32, low / len(cuts), top_value / len(cuts))
        loudness = loudness * jnp.repeat(jnp.exp(steps), extent[dim] // parts).reshape((-1,) + (1,) * (len(extent) - 1 - dim))
    return loudness


def gaussian(key, extent, scale, bound, shards=(), held_as=jnp.bfloat16):
    array = scale * jax.random.normal(key, extent, jnp.float32)
    if shards:
        array = array * levels(key, extent, shards, -0.22, 0.18)
    return jnp.clip(array, -bound, bound).astype(held_as)


def setup_inputs(seed: int = 0, part: int = 0) -> dict:
    key_of = jax.random.split(jax.random.key(seed), 12)
    part_splits = jax.random.split(jax.random.fold_in(key_of[11], part), 12)
    return {
        "pair_input": gaussian(part_splits[0], (N, N, C), 1.0, 6.0, ((0, 8),)),
        "outgoing_weights": gaussian(key_of[1], (4, C, H), C ** -0.5, 0.5, ((2, 2),)),
        "outgoing_gate": gaussian(key_of[2], (C, C), C ** -0.5, 0.5, ((1, 2),)),
        "outgoing_output": gaussian(key_of[3], (H, C), H ** -0.5, 0.5, ((0, 2),)),
        "incoming_weights": gaussian(key_of[4], (4, C, H), C ** -0.5, 0.5, ((2, 2),)),
        "incoming_gate": gaussian(key_of[5], (C, C), C ** -0.5, 0.5, ((1, 2),)),
        "incoming_output": gaussian(key_of[6], (H, C), H ** -0.5, 0.5, ((0, 2),)),
        "distogram_head": gaussian(key_of[7], (C, BINS), C ** -0.5, 0.5),
        "distance_bins": set_ends(jax.random.randint(part_splits[8], (N, N), 0, BINS), jax.random.fold_in(part_splits[8], 1), 0, BINS - 1).astype(jnp.int32),
        "chain_index": draw_chain_index(jax.random.fold_in(jax.random.fold_in(key_of[11], part), 71), part),
        "chain_swap": draw_chain_swap(jax.random.fold_in(jax.random.fold_in(key_of[11], part), 71), part),
    }


epsilon = 1e-05

def normalize(values):
    center = lax.optimization_barrier(jnp.mean(values, axis=-1, keepdims=True))
    centred = values - center
    inverse = lax.rsqrt(lax.optimization_barrier(jnp.mean(centred * centred, axis=-1, keepdims=True)) + epsilon)
    return (centred * inverse, inverse)

def wide(values):
    return values.astype(jnp.float32)

def triangle_forward(pair_rows, weights, gate_w, out_w, roles):
    value_left, gate_left, value_right, gate_right = roles
    pair_float = wide(pair_rows)
    pair_hat, pair_inverse = normalize(pair_float)
    normed = pair_hat.astype(jnp.bfloat16)
    projected = jnp.einsum('rnc,qch->qhrn', wide(normed), wide(weights))
    local_side = (jax.nn.sigmoid(projected[gate_left]) * projected[value_left]).astype(jnp.bfloat16)
    remote_side = (jax.nn.sigmoid(projected[gate_right]) * projected[value_right]).astype(jnp.bfloat16)
    mixed_sum = jnp.einsum('hik,hjk->hij', wide(local_side), wide(remote_side))
    mean_hidden = lax.optimization_barrier(jnp.mean(mixed_sum, axis=0))
    inv_hidden = lax.rsqrt(lax.optimization_barrier(jnp.mean(mixed_sum * mixed_sum, axis=0)) - mean_hidden * mean_hidden + epsilon)
    mixed_hat = (mixed_sum - mean_hidden) * inv_hidden
    mixed_norm = mixed_hat.astype(jnp.bfloat16)
    update_full = jnp.einsum('hrn,hc->rnc', wide(mixed_norm), wide(out_w))
    gating = jax.nn.sigmoid(jnp.einsum('rnc,cd->rnd', wide(normed), wide(gate_w)))
    result = (pair_float + gating * update_full).astype(jnp.bfloat16)
    stored = (pair_hat, pair_inverse, normed, projected, local_side, remote_side, mixed_hat, inv_hidden, mixed_norm, update_full, gating)
    return (result, stored)

def triangle_backward(grad_out, stored, weights, gate_w, out_w, roles):
    pair_hat, pair_inverse, normed, projected, local_side, remote_side, mixed_hat, inv_hidden, mixed_norm, update_full, gating = stored
    value_left, gate_left, value_right, gate_right = roles
    grad_gate = (grad_out * update_full * gating * (1.0 - gating)).astype(jnp.bfloat16)
    grad_update = (grad_out * gating).astype(jnp.bfloat16)
    d_gate = jnp.einsum('rnc,rnd->cd', wide(normed), wide(grad_gate))
    d_output = jnp.einsum('hrn,rnc->hc', wide(mixed_norm), wide(grad_update))
    grad_norm = jnp.einsum('rnc,hc->hrn', wide(grad_update), wide(out_w))
    grad_mixed = (inv_hidden * (grad_norm - lax.optimization_barrier(jnp.mean(grad_norm, axis=0)) - mixed_hat * lax.optimization_barrier(jnp.mean(grad_norm * mixed_hat, axis=0)))).astype(jnp.bfloat16)
    grad_local = jnp.einsum('hij,hjk->hik', wide(grad_mixed), wide(remote_side))
    grad_remote = jnp.einsum('hij,hik->hjk', wide(grad_mixed), wide(local_side))
    sigmoid_left = jax.nn.sigmoid(projected[gate_left])
    sigmoid_right = jax.nn.sigmoid(projected[gate_right])
    pieces = [None, None, None, None]
    pieces[value_left] = grad_local * sigmoid_left
    pieces[gate_left] = grad_local * projected[value_left] * sigmoid_left * (1.0 - sigmoid_left)
    pieces[value_right] = grad_remote * sigmoid_right
    pieces[gate_right] = grad_remote * projected[value_right] * sigmoid_right * (1.0 - sigmoid_right)
    grad_proj = jnp.stack(pieces).astype(jnp.bfloat16)
    d_weights = jnp.einsum('rnc,qhrn->qch', wide(normed), wide(grad_proj))
    grad_normed = jnp.einsum('qhrn,qch->rnc', wide(grad_proj), wide(weights))
    grad_normed = grad_normed + jnp.einsum('rnd,cd->rnc', wide(grad_gate), wide(gate_w))
    grad_in = grad_out + pair_inverse * (grad_normed - lax.optimization_barrier(jnp.mean(grad_normed, axis=-1, keepdims=True)) - pair_hat * lax.optimization_barrier(jnp.mean(grad_normed * pair_hat, axis=-1, keepdims=True)))
    return (grad_in, d_weights, d_gate, d_output)

def residue_permutation(chain_index, chain_swap):
    chains = chain_swap.shape[0]
    chain_ids = jnp.arange(chains, dtype=jnp.int32)
    starts = lax.optimization_barrier(jnp.sum((chain_index[None, :] < chain_ids[:, None]).astype(jnp.int32), axis=1))
    mapped_starts = lax.optimization_barrier(jnp.sum((chain_swap[:, None] == chain_ids[None, :]).astype(jnp.int32) * starts[None, :], axis=1))
    member = (chain_index[:, None] == chain_ids[None, :]).astype(jnp.int32)
    own_start = lax.optimization_barrier(jnp.sum(member * starts[None, :], axis=1))
    new_start = lax.optimization_barrier(jnp.sum(member * mapped_starts[None, :], axis=1))
    positions = jnp.arange(chain_index.shape[0], dtype=jnp.int32)
    return (positions - own_start + new_start).astype(jnp.int32)

def reference(pair_input, outgoing_weights, outgoing_gate, outgoing_output, incoming_weights, incoming_gate, incoming_output, distogram_head, distance_bins, chain_index, chain_swap):
    middle, stored_out = triangle_forward(pair_input, outgoing_weights, outgoing_gate, outgoing_output, (0, 1, 2, 3))
    middle_t = jnp.transpose(middle, (1, 0, 2))
    final_t, stored_in = triangle_forward(middle_t, incoming_weights, incoming_gate, incoming_output, (2, 3, 0, 1))
    final_rows = jnp.transpose(final_t, (1, 0, 2))
    permuted = residue_permutation(chain_index, chain_swap)
    target = jnp.take(jnp.take(distance_bins, permuted, axis=0), permuted, axis=1)
    row_logits = jnp.einsum('ijc,cb->ijb', wide(final_rows), wide(distogram_head))
    logits = row_logits + jnp.transpose(row_logits, (1, 0, 2))
    log_total = jnp.log(lax.optimization_barrier(jnp.sum(jnp.exp(logits), axis=-1, keepdims=True)))
    bins = distogram_head.shape[1]
    onehot = (target[:, :, None] == jnp.arange(bins, dtype=jnp.int32)[None, None, :]).astype(jnp.float32)
    grad_logits = (jnp.exp(logits - log_total) - onehot).astype(jnp.bfloat16)
    d_head = jnp.einsum('ijc,ijb->cb', wide(final_rows), wide(grad_logits))
    d_head = d_head + jnp.einsum('ijc,ijb->cb', wide(final_t), wide(grad_logits))
    grad_rows = jnp.einsum('ijb,cb->ijc', wide(grad_logits), wide(distogram_head))
    grad_t = grad_rows + jnp.transpose(grad_rows, (1, 0, 2))
    grad_mid_t, dw_in, dg_in, do_in = triangle_backward(grad_t, stored_in, incoming_weights, incoming_gate, incoming_output, (2, 3, 0, 1))
    grad_mid = jnp.transpose(grad_mid_t, (1, 0, 2))
    pair_grad, dw_out, dg_out, do_out = triangle_backward(grad_mid, stored_out, outgoing_weights, outgoing_gate, outgoing_output, (0, 1, 2, 3))
    inv_count = 1.0 / pair_input.shape[0]
    return (pair_grad, dw_out * inv_count, dg_out * inv_count, do_out * inv_count, dw_in * inv_count, dg_in * inv_count, do_in * inv_count, d_head * inv_count)
```

```python
import jax
import jax.numpy as jnp
from jax import lax
from jax.sharding import PartitionSpec as P

H = 128


epsilon = 1e-05


def normalize(values):
    center = jnp.mean(values, axis=-1, keepdims=True)
    centred = values - center
    inverse = lax.rsqrt(jnp.mean(centred * centred, axis=-1, keepdims=True) + epsilon)
    return (centred * inverse, inverse)


def triangle_forward(pair_rows, weights, gate_w, out_w, roles):
    value_left, gate_left, value_right, gate_right = roles
    pair_float = pair_rows.astype(jnp.float32)
    pair_hat, pair_inverse = normalize(pair_float)
    normed = pair_hat.astype(jnp.bfloat16)
    projected = jnp.einsum("rnc,qch->qhrn", normed, weights, preferred_element_type=jnp.float32)
    local_side = (jax.nn.sigmoid(projected[gate_left]) * projected[value_left]).astype(jnp.bfloat16)
    remote_side = (jax.nn.sigmoid(projected[gate_right]) * projected[value_right]).astype(
        jnp.bfloat16
    )
    remote_all = lax.all_gather(remote_side, "dap", axis=1, tiled=True)
    mixed_sum = jnp.einsum(
        "hik,hjk->hij", local_side, remote_all, preferred_element_type=jnp.float32
    )
    total_one, total_two = lax.psum(
        (jnp.sum(mixed_sum, axis=0), jnp.sum(mixed_sum * mixed_sum, axis=0)), "rep"
    )
    mean_hidden = total_one / H
    inv_hidden = lax.rsqrt(total_two / H - mean_hidden * mean_hidden + epsilon)
    mixed_hat = (mixed_sum - mean_hidden) * inv_hidden
    mixed_norm = mixed_hat.astype(jnp.bfloat16)
    partial_out = jnp.einsum("hrn,hc->rnc", mixed_norm, out_w, preferred_element_type=jnp.float32)
    update_half = lax.psum_scatter(partial_out, "rep", scatter_dimension=2, tiled=True)
    gating = jax.nn.sigmoid(
        jnp.einsum("rnc,cd->rnd", normed, gate_w, preferred_element_type=jnp.float32)
    )
    update_full = lax.all_gather(gating * update_half, "rep", axis=2, tiled=True)
    result = (pair_float + update_full).astype(jnp.bfloat16)
    stored = (
        pair_hat,
        pair_inverse,
        normed,
        projected,
        local_side,
        remote_all,
        mixed_hat,
        inv_hidden,
        mixed_norm,
        update_half,
        gating,
    )
    return (result, stored)


def triangle_backward(grad_out, stored, weights, gate_w, out_w, roles):
    (
        pair_hat,
        pair_inverse,
        normed,
        projected,
        local_side,
        carried,
        mixed_hat,
        inv_hidden,
        mixed_norm,
        update_half,
        gating,
    ) = stored
    value_left, gate_left, value_right, gate_right = roles
    width_half = gate_w.shape[1]
    rep_index = lax.axis_index("rep")
    grad_half = lax.dynamic_slice_in_dim(grad_out, rep_index * width_half, width_half, 2)
    grad_gate = (grad_half * update_half * gating * (1.0 - gating)).astype(jnp.bfloat16)
    update_grad_half = (grad_half * gating).astype(jnp.bfloat16)
    grad_update = lax.all_gather(update_grad_half, "rep", axis=2, tiled=True)
    d_gate = jnp.einsum("rnc,rnd->cd", normed, grad_gate, preferred_element_type=jnp.float32)
    d_output = jnp.einsum(
        "hrn,rnc->hc", mixed_norm, grad_update, preferred_element_type=jnp.float32
    )
    grad_norm = jnp.einsum("rnc,hc->hrn", grad_update, out_w, preferred_element_type=jnp.float32)
    sum_one, sum_two = lax.psum(
        (jnp.sum(grad_norm, axis=0), jnp.sum(grad_norm * mixed_hat, axis=0)), "rep"
    )
    grad_mixed = (inv_hidden * (grad_norm - sum_one / H - mixed_hat * (sum_two / H))).astype(
        jnp.bfloat16
    )
    grad_local = jnp.einsum("hij,hjk->hik", grad_mixed, carried, preferred_element_type=jnp.float32)
    swapped = lax.psum_scatter(
        jnp.einsum(
            "hij,hik->jhk", grad_mixed, local_side, preferred_element_type=jnp.float32
        ).astype(jnp.bfloat16),
        "dap",
        scatter_dimension=0,
        tiled=True,
    ).astype(jnp.float32)
    grad_remote = jnp.swapaxes(swapped, 0, 1)
    sigmoid_left = jax.nn.sigmoid(projected[gate_left])
    sigmoid_right = jax.nn.sigmoid(projected[gate_right])
    pieces = [None, None, None, None]
    pieces[value_left] = grad_local * sigmoid_left
    pieces[gate_left] = grad_local * projected[value_left] * sigmoid_left * (1.0 - sigmoid_left)
    pieces[value_right] = grad_remote * sigmoid_right
    pieces[gate_right] = (
        grad_remote * projected[value_right] * sigmoid_right * (1.0 - sigmoid_right)
    )
    grad_proj = jnp.stack(pieces).astype(jnp.bfloat16)
    d_weights = jnp.einsum("rnc,qhrn->qch", normed, grad_proj, preferred_element_type=jnp.float32)
    partial_sum = jnp.einsum(
        "qhrn,qch->rnc", grad_proj, weights, preferred_element_type=jnp.float32
    )
    partial_sum = partial_sum + jnp.einsum(
        "rnd,cd->rnc", grad_gate, gate_w, preferred_element_type=jnp.float32
    )
    grad_normed = lax.psum(partial_sum.astype(jnp.bfloat16), "rep").astype(jnp.float32)
    grad_in = grad_out + pair_inverse * (
        grad_normed
        - jnp.mean(grad_normed, axis=-1, keepdims=True)
        - pair_hat * jnp.mean(grad_normed * pair_hat, axis=-1, keepdims=True)
    )
    return (grad_in, d_weights, d_gate, d_output)


def residue_permutation(chain_index, chain_swap):
    chains = chain_swap.shape[0]
    chain_ids = jnp.arange(chains, dtype=jnp.int32)
    starts = jnp.sum((chain_index[None, :] < chain_ids[:, None]).astype(jnp.int32), axis=1)
    mapped_starts = jnp.sum(
        (chain_swap[:, None] == chain_ids[None, :]).astype(jnp.int32) * starts[None, :], axis=1
    )
    member = (chain_index[:, None] == chain_ids[None, :]).astype(jnp.int32)
    own_start = jnp.sum(member * starts[None, :], axis=1)
    new_start = jnp.sum(member * mapped_starts[None, :], axis=1)
    positions = jnp.arange(chain_index.shape[0], dtype=jnp.int32)
    return positions - own_start + new_start


def per_device(
    pair_input,
    outgoing_weights,
    outgoing_gate,
    outgoing_output,
    incoming_weights,
    incoming_gate,
    incoming_output,
    distogram_head,
    distance_bins,
    chain_index,
    chain_swap,
):
    row_count = pair_input.shape[0]
    residues = pair_input.shape[1]
    middle, stored_out = triangle_forward(
        pair_input, outgoing_weights, outgoing_gate, outgoing_output, (0, 1, 2, 3)
    )
    middle_t = jnp.swapaxes(
        lax.all_to_all(middle, "dap", split_axis=1, concat_axis=0, tiled=True), 0, 1
    )
    final_t, stored_in = triangle_forward(
        middle_t, incoming_weights, incoming_gate, incoming_output, (2, 3, 0, 1)
    )
    final_rows = jnp.swapaxes(
        lax.all_to_all(final_t, "dap", split_axis=1, concat_axis=0, tiled=True), 0, 1
    )
    half_rows = row_count // lax.axis_size("rep")
    rep_index = lax.axis_index("rep")
    own_rows = lax.dynamic_slice_in_dim(final_rows, rep_index * half_rows, half_rows, 0)
    own_cols = lax.dynamic_slice_in_dim(final_t, rep_index * half_rows, half_rows, 0)
    two_views = jnp.stack([own_rows, own_cols])
    view_logits = jnp.einsum(
        "srnc,cb->srnb", two_views, distogram_head, preferred_element_type=jnp.float32
    )
    logits = view_logits[0] + view_logits[1]
    permuted = residue_permutation(chain_index, chain_swap)
    row_ids = (
        lax.axis_index("dap") * row_count
        + rep_index * half_rows
        + jnp.arange(half_rows, dtype=jnp.int32)
    )
    target = jnp.take(
        jnp.take(distance_bins, jnp.take(permuted, row_ids), axis=0), permuted, axis=1
    )
    log_total = jnp.log(jnp.sum(jnp.exp(logits), axis=-1, keepdims=True))
    bins = distogram_head.shape[1]
    onehot = (target[:, :, None] == jnp.arange(bins, dtype=jnp.int32)[None, None, :]).astype(
        jnp.float32
    )
    grad_logits = (jnp.exp(logits - log_total) - onehot).astype(jnp.bfloat16)
    d_head = jnp.einsum("srnc,rnb->cb", two_views, grad_logits, preferred_element_type=jnp.float32)
    grad_half = jnp.einsum(
        "rnb,cb->rnc", grad_logits, distogram_head, preferred_element_type=jnp.float32
    )
    grad_rows = lax.all_gather(grad_half.astype(jnp.bfloat16), "rep", axis=0, tiled=True).astype(
        grad_half.dtype
    )
    mirrored = jnp.swapaxes(
        lax.all_to_all(
            grad_rows.astype(jnp.bfloat16), "dap", split_axis=1, concat_axis=0, tiled=True
        ).astype(grad_rows.dtype),
        0,
        1,
    )
    grad_t = grad_rows + mirrored
    grad_mid_t, dw_in, dg_in, do_in = triangle_backward(
        grad_t, stored_in, incoming_weights, incoming_gate, incoming_output, (2, 3, 0, 1)
    )
    grad_mid = jnp.swapaxes(
        lax.all_to_all(
            grad_mid_t.astype(jnp.bfloat16), "dap", split_axis=1, concat_axis=0, tiled=True
        ).astype(grad_mid_t.dtype),
        0,
        1,
    )
    pair_grad, dw_out, dg_out, do_out = triangle_backward(
        grad_mid, stored_out, outgoing_weights, outgoing_gate, outgoing_output, (0, 1, 2, 3)
    )
    grad_sums = (
        lax.psum(dw_out.astype(jnp.bfloat16), "dap").astype(jnp.float32),
        lax.psum(dg_out.astype(jnp.bfloat16), "dap").astype(jnp.float32),
        lax.psum(do_out.astype(jnp.bfloat16), "dap").astype(jnp.float32),
        lax.psum(dw_in.astype(jnp.bfloat16), "dap").astype(jnp.float32),
        lax.psum(dg_in.astype(jnp.bfloat16), "dap").astype(jnp.float32),
        lax.psum(do_in.astype(jnp.bfloat16), "dap").astype(jnp.float32),
    )
    head_total = lax.psum(d_head, ("dap", "rep"))
    inv_count = 1.0 / residues
    return (
        pair_grad,
        grad_sums[0] * inv_count,
        grad_sums[1] * inv_count,
        grad_sums[2] * inv_count,
        grad_sums[3] * inv_count,
        grad_sums[4] * inv_count,
        grad_sums[5] * inv_count,
        head_total * inv_count,
    )


def gather_part(pair_input, matrices, dap, rep):
    rows, residues, channels = pair_input.shape
    half_rows = rows // rep
    rep_index = lax.axis_index("rep")
    dap_index = lax.axis_index("dap")
    own_rows = lax.dynamic_slice_in_dim(pair_input, rep_index * half_rows, half_rows, 0)
    stack = jnp.stack(matrices)
    count, depth, width = stack.shape
    share = depth // dap
    own_share = lax.dynamic_slice_in_dim(stack, dap_index * share, share, 1)
    pair_size = half_rows * residues * channels
    packed = jnp.concatenate(
        [own_rows.reshape(-1, channels), own_share.reshape(-1, channels)], axis=0
    )
    everything = lax.all_gather(packed, ("dap", "rep"), axis=0, tiled=False)
    split = pair_size // channels
    pair_all = everything[:, :split].reshape(dap * rows, residues, channels)
    tail = everything[:, split:].reshape(dap, rep, count, share, width)
    mats = jnp.transpose(tail, (2, 0, 3, 1, 4)).reshape(count, depth, rep * width)
    return (pair_all, mats)


def forward_whole(pair_rows, weights, gate_w, out_t, roles):
    value_left, gate_left, value_right, gate_right = roles
    pair_float = pair_rows.astype(jnp.float32)
    pair_hat, pair_inverse = normalize(pair_float)
    normed = pair_hat.astype(jnp.bfloat16)
    projected = jnp.einsum("rnc,qch->qhrn", normed, weights, preferred_element_type=jnp.float32)
    left = (jax.nn.sigmoid(projected[gate_left]) * projected[value_left]).astype(jnp.bfloat16)
    right = (jax.nn.sigmoid(projected[gate_right]) * projected[value_right]).astype(jnp.bfloat16)
    mixed_sum = jnp.einsum("hik,hjk->hij", left, right, preferred_element_type=jnp.float32)
    mean_hidden = jnp.mean(mixed_sum, axis=0)
    inv_hidden = lax.rsqrt(
        jnp.mean(mixed_sum * mixed_sum, axis=0) - mean_hidden * mean_hidden + epsilon
    )
    mixed_hat = (mixed_sum - mean_hidden) * inv_hidden
    mixed_norm = mixed_hat.astype(jnp.bfloat16)
    update = jnp.einsum("hrn,ch->rnc", mixed_norm, out_t, preferred_element_type=jnp.float32)
    gating = jax.nn.sigmoid(
        jnp.einsum("rnc,cd->rnd", normed, gate_w, preferred_element_type=jnp.float32)
    )
    result = (pair_float + gating * update).astype(jnp.bfloat16)
    stored = (
        pair_hat,
        pair_inverse,
        normed,
        projected,
        left,
        right,
        mixed_hat,
        inv_hidden,
        mixed_norm,
        update,
        gating,
    )
    return (result, stored)


def backward_whole(grad_out, stored, weights, gate_w, out_t, roles):
    (
        pair_hat,
        pair_inverse,
        normed,
        projected,
        left,
        right,
        mixed_hat,
        inv_hidden,
        mixed_norm,
        update,
        gating,
    ) = stored
    value_left, gate_left, value_right, gate_right = roles
    grad_gate = (grad_out * update * gating * (1.0 - gating)).astype(jnp.bfloat16)
    grad_update = (grad_out * gating).astype(jnp.bfloat16)
    d_gate = jnp.einsum("rnc,rnd->cd", normed, grad_gate, preferred_element_type=jnp.float32)
    d_output = jnp.einsum(
        "hrn,rnc->hc", mixed_norm, grad_update, preferred_element_type=jnp.float32
    )
    grad_norm = jnp.einsum("rnc,ch->hrn", grad_update, out_t, preferred_element_type=jnp.float32)
    grad_mixed = (
        inv_hidden
        * (
            grad_norm
            - jnp.mean(grad_norm, axis=0)
            - mixed_hat * jnp.mean(grad_norm * mixed_hat, axis=0)
        )
    ).astype(jnp.bfloat16)
    grad_left = jnp.einsum("hij,hjk->hik", grad_mixed, right, preferred_element_type=jnp.float32)
    grad_right = jnp.einsum("hij,hik->hjk", grad_mixed, left, preferred_element_type=jnp.float32)
    sigmoid_left = jax.nn.sigmoid(projected[gate_left])
    sigmoid_right = jax.nn.sigmoid(projected[gate_right])
    pieces = [None, None, None, None]
    pieces[value_left] = grad_left * sigmoid_left
    pieces[gate_left] = grad_left * projected[value_left] * sigmoid_left * (1.0 - sigmoid_left)
    pieces[value_right] = grad_right * sigmoid_right
    pieces[gate_right] = grad_right * projected[value_right] * sigmoid_right * (1.0 - sigmoid_right)
    grad_proj = jnp.stack(pieces).astype(jnp.bfloat16)
    d_weights = jnp.einsum("rnc,qhrn->qch", normed, grad_proj, preferred_element_type=jnp.float32)
    grad_normed = jnp.einsum(
        "qhrn,qch->rnc", grad_proj, weights, preferred_element_type=jnp.float32
    )
    grad_normed = grad_normed + jnp.einsum(
        "rnd,cd->rnc", grad_gate, gate_w, preferred_element_type=jnp.float32
    )
    grad_in = grad_out + pair_inverse * (
        grad_normed
        - jnp.mean(grad_normed, axis=-1, keepdims=True)
        - pair_hat * jnp.mean(grad_normed * pair_hat, axis=-1, keepdims=True)
    )
    return (grad_in, d_weights, d_gate, d_output)


def whole_part(dap, rep):
    def run(
        pair_input,
        outgoing_weights,
        outgoing_gate,
        outgoing_output,
        incoming_weights,
        incoming_gate,
        incoming_output,
        distogram_head,
        distance_bins,
        chain_index,
        chain_swap,
    ):
        rows = pair_input.shape[0]
        matrices = [outgoing_weights[q] for q in range(4)] + [outgoing_gate, outgoing_output.T]
        matrices += [incoming_weights[q] for q in range(4)] + [incoming_gate, incoming_output.T]
        pair_all, mats = gather_part(pair_input, matrices, dap, rep)
        w_out, g_out, o_out = mats[0:4], mats[4], mats[5]
        w_in, g_in, o_in = mats[6:10], mats[10], mats[11]
        middle, stored_out = forward_whole(pair_all, w_out, g_out, o_out, (0, 1, 2, 3))
        middle_t = jnp.swapaxes(middle, 0, 1)
        final_t, stored_in = forward_whole(middle_t, w_in, g_in, o_in, (2, 3, 0, 1))
        permuted = residue_permutation(chain_index, chain_swap)
        bins = distogram_head.shape[1]
        ids = jnp.arange(bins, dtype=jnp.int32)
        residues = pair_all.shape[1]
        positions = jnp.arange(residues, dtype=jnp.int32)
        mover = (permuted[:, None] == positions[None, :]).astype(jnp.bfloat16)
        moved = jnp.einsum(
            "ia,ab,jb->ij",
            mover,
            distance_bins.astype(jnp.bfloat16),
            mover,
            preferred_element_type=jnp.float32,
        )
        target = moved.astype(jnp.int32)
        half_logits = jnp.einsum(
            "jic,cb->jib", final_t, distogram_head, preferred_element_type=jnp.float32
        )
        logits = half_logits + jnp.swapaxes(half_logits, 0, 1)
        log_total = jnp.log(jnp.sum(jnp.exp(logits), axis=-1, keepdims=True))
        prob = jnp.exp(logits - log_total)
        onehot_rows = (target[:, :, None] == ids[None, None, :]).astype(jnp.float32)
        onehot_cols = (target.T[:, :, None] == ids[None, None, :]).astype(jnp.float32)
        glog_rows = (prob - onehot_rows).astype(jnp.bfloat16)
        glog_cols = (prob - onehot_cols).astype(jnp.bfloat16)
        both = jnp.concatenate([glog_rows, glog_cols], axis=-1)
        heads = jnp.concatenate([distogram_head, distogram_head], axis=1)
        d_both = jnp.einsum("jic,jib->cb", final_t, both, preferred_element_type=jnp.float32)
        d_head = d_both[:, :bins] + d_both[:, bins:]
        grad_t = jnp.einsum("jib,cb->jic", both, heads, preferred_element_type=jnp.float32)
        grad_mid_t, dw_in, dg_in, do_in = backward_whole(
            grad_t, stored_in, w_in, g_in, o_in, (2, 3, 0, 1)
        )
        grad_mid = jnp.swapaxes(grad_mid_t, 0, 1)
        pair_grad, dw_out, dg_out, do_out = backward_whole(
            grad_mid, stored_out, w_out, g_out, o_out, (0, 1, 2, 3)
        )
        scale = 1.0 / residues
        half = outgoing_weights.shape[2]
        start = lax.axis_index("rep") * half

        def mine(values, axis):
            return lax.dynamic_slice_in_dim(values, start, half, axis) * scale

        return (
            lax.dynamic_slice_in_dim(pair_grad, lax.axis_index("dap") * rows, rows, 0),
            mine(dw_out, 2),
            mine(dg_out, 1),
            mine(do_out, 0),
            mine(dw_in, 2),
            mine(dg_in, 1),
            mine(do_in, 0),
            d_head * scale,
        )

    return run


def solution(mesh):
    dap, rep = mesh.shape["dap"], mesh.shape["rep"]

    def plan(*arrays):
        residues, channels = arrays[0].shape[1], arrays[0].shape[2]
        small = residues <= 64 and (arrays[0].shape[0] % rep) == 0 and channels % dap == 0
        return (whole_part(dap, rep) if small else per_device)(*arrays)

    return jax.shard_map(
        plan,
        mesh=mesh,
        in_specs=(
            P(("groups", "dap"), None, None),
            P(None, None, "rep"),
            P(None, "rep"),
            P("rep", None),
            P(None, None, "rep"),
            P(None, "rep"),
            P("rep", None),
            P(),
            P("groups", None),
            P("groups"),
            P("groups"),
        ),
        out_specs=(
            P(("groups", "dap"), None, None),
            P("groups", None, "rep"),
            P("groups", "rep"),
            P(("groups", "rep"), None),
            P("groups", None, "rep"),
            P("groups", "rep"),
            P(("groups", "rep"), None),
            P("groups", None),
        ),
        check_vma=False,
    )
```

```python
import jax
import jax.numpy as jnp
from jax import lax
from jax.experimental import pallas as pl
from jax.experimental.pallas import tpu as pltpu
from jax.sharding import PartitionSpec as P

H = 128


epsilon = 1e-05


def normalize(values):
    center = jnp.mean(values, axis=-1, keepdims=True)
    centred = values - center
    inverse = lax.rsqrt(jnp.mean(centred * centred, axis=-1, keepdims=True) + epsilon)
    return (centred * inverse, inverse)


def triangle_forward(pair_rows, weights, gate_w, out_w, roles):
    value_left, gate_left, value_right, gate_right = roles
    pair_float = pair_rows.astype(jnp.float32)
    pair_hat, pair_inverse = normalize(pair_float)
    normed = pair_hat.astype(jnp.bfloat16)
    projected = jnp.einsum("rnc,qch->qhrn", normed, weights, preferred_element_type=jnp.float32)
    local_side = (jax.nn.sigmoid(projected[gate_left]) * projected[value_left]).astype(jnp.bfloat16)
    remote_side = (jax.nn.sigmoid(projected[gate_right]) * projected[value_right]).astype(
        jnp.bfloat16
    )
    remote_all = lax.all_gather(remote_side, "dap", axis=1, tiled=True)
    mixed_sum = jnp.einsum(
        "hik,hjk->hij", local_side, remote_all, preferred_element_type=jnp.float32
    )
    total_one, total_two = lax.psum(
        (jnp.sum(mixed_sum, axis=0), jnp.sum(mixed_sum * mixed_sum, axis=0)), "rep"
    )
    mean_hidden = total_one / H
    inv_hidden = lax.rsqrt(total_two / H - mean_hidden * mean_hidden + epsilon)
    mixed_hat = (mixed_sum - mean_hidden) * inv_hidden
    mixed_norm = mixed_hat.astype(jnp.bfloat16)
    partial_out = jnp.einsum("hrn,hc->rnc", mixed_norm, out_w, preferred_element_type=jnp.float32)
    update_half = lax.psum_scatter(partial_out, "rep", scatter_dimension=2, tiled=True)
    gating = jax.nn.sigmoid(
        jnp.einsum("rnc,cd->rnd", normed, gate_w, preferred_element_type=jnp.float32)
    )
    update_full = lax.all_gather(gating * update_half, "rep", axis=2, tiled=True)
    result = (pair_float + update_full).astype(jnp.bfloat16)
    stored = (
        pair_hat,
        pair_inverse,
        normed,
        projected,
        local_side,
        remote_all,
        mixed_hat,
        inv_hidden,
        mixed_norm,
        update_half,
        gating,
    )
    return (result, stored)


def triangle_backward(grad_out, stored, weights, gate_w, out_w, roles):
    (
        pair_hat,
        pair_inverse,
        normed,
        projected,
        local_side,
        carried,
        mixed_hat,
        inv_hidden,
        mixed_norm,
        update_half,
        gating,
    ) = stored
    value_left, gate_left, value_right, gate_right = roles
    width_half = gate_w.shape[1]
    rep_index = lax.axis_index("rep")
    grad_half = lax.dynamic_slice_in_dim(grad_out, rep_index * width_half, width_half, 2)
    grad_gate = (grad_half * update_half * gating * (1.0 - gating)).astype(jnp.bfloat16)
    update_grad_half = (grad_half * gating).astype(jnp.bfloat16)
    grad_update = lax.all_gather(update_grad_half, "rep", axis=2, tiled=True)
    d_gate = jnp.einsum("rnc,rnd->cd", normed, grad_gate, preferred_element_type=jnp.float32)
    d_output = jnp.einsum(
        "hrn,rnc->hc", mixed_norm, grad_update, preferred_element_type=jnp.float32
    )
    grad_norm = jnp.einsum("rnc,hc->hrn", grad_update, out_w, preferred_element_type=jnp.float32)
    sum_one, sum_two = lax.psum(
        (jnp.sum(grad_norm, axis=0), jnp.sum(grad_norm * mixed_hat, axis=0)), "rep"
    )
    grad_mixed = (inv_hidden * (grad_norm - sum_one / H - mixed_hat * (sum_two / H))).astype(
        jnp.bfloat16
    )
    grad_local = jnp.einsum("hij,hjk->hik", grad_mixed, carried, preferred_element_type=jnp.float32)
    swapped = lax.psum_scatter(
        jnp.einsum(
            "hij,hik->jhk", grad_mixed, local_side, preferred_element_type=jnp.float32
        ).astype(jnp.bfloat16),
        "dap",
        scatter_dimension=0,
        tiled=True,
    ).astype(jnp.float32)
    grad_remote = jnp.swapaxes(swapped, 0, 1)
    sigmoid_left = jax.nn.sigmoid(projected[gate_left])
    sigmoid_right = jax.nn.sigmoid(projected[gate_right])
    pieces = [None, None, None, None]
    pieces[value_left] = grad_local * sigmoid_left
    pieces[gate_left] = grad_local * projected[value_left] * sigmoid_left * (1.0 - sigmoid_left)
    pieces[value_right] = grad_remote * sigmoid_right
    pieces[gate_right] = (
        grad_remote * projected[value_right] * sigmoid_right * (1.0 - sigmoid_right)
    )
    grad_proj = jnp.stack(pieces).astype(jnp.bfloat16)
    d_weights = jnp.einsum("rnc,qhrn->qch", normed, grad_proj, preferred_element_type=jnp.float32)
    partial_sum = jnp.einsum(
        "qhrn,qch->rnc", grad_proj, weights, preferred_element_type=jnp.float32
    )
    partial_sum = partial_sum + jnp.einsum(
        "rnd,cd->rnc", grad_gate, gate_w, preferred_element_type=jnp.float32
    )
    grad_normed = lax.psum(partial_sum.astype(jnp.bfloat16), "rep").astype(jnp.float32)
    grad_in = grad_out + pair_inverse * (
        grad_normed
        - jnp.mean(grad_normed, axis=-1, keepdims=True)
        - pair_hat * jnp.mean(grad_normed * pair_hat, axis=-1, keepdims=True)
    )
    return (grad_in, d_weights, d_gate, d_output)


def residue_permutation(chain_index, chain_swap):
    chains = chain_swap.shape[0]
    chain_ids = jnp.arange(chains, dtype=jnp.int32)
    starts = jnp.sum((chain_index[None, :] < chain_ids[:, None]).astype(jnp.int32), axis=1)
    mapped_starts = jnp.sum(
        (chain_swap[:, None] == chain_ids[None, :]).astype(jnp.int32) * starts[None, :], axis=1
    )
    member = (chain_index[:, None] == chain_ids[None, :]).astype(jnp.int32)
    own_start = jnp.sum(member * starts[None, :], axis=1)
    new_start = jnp.sum(member * mapped_starts[None, :], axis=1)
    positions = jnp.arange(chain_index.shape[0], dtype=jnp.int32)
    return positions - own_start + new_start


def per_device(
    pair_input,
    outgoing_weights,
    outgoing_gate,
    outgoing_output,
    incoming_weights,
    incoming_gate,
    incoming_output,
    distogram_head,
    distance_bins,
    chain_index,
    chain_swap,
):
    row_count = pair_input.shape[0]
    residues = pair_input.shape[1]
    middle, stored_out = triangle_forward(
        pair_input, outgoing_weights, outgoing_gate, outgoing_output, (0, 1, 2, 3)
    )
    middle_t = jnp.swapaxes(
        lax.all_to_all(middle, "dap", split_axis=1, concat_axis=0, tiled=True), 0, 1
    )
    final_t, stored_in = triangle_forward(
        middle_t, incoming_weights, incoming_gate, incoming_output, (2, 3, 0, 1)
    )
    final_rows = jnp.swapaxes(
        lax.all_to_all(final_t, "dap", split_axis=1, concat_axis=0, tiled=True), 0, 1
    )
    half_rows = row_count // lax.axis_size("rep")
    rep_index = lax.axis_index("rep")
    own_rows = lax.dynamic_slice_in_dim(final_rows, rep_index * half_rows, half_rows, 0)
    own_cols = lax.dynamic_slice_in_dim(final_t, rep_index * half_rows, half_rows, 0)
    two_views = jnp.stack([own_rows, own_cols])
    view_logits = jnp.einsum(
        "srnc,cb->srnb", two_views, distogram_head, preferred_element_type=jnp.float32
    )
    logits = view_logits[0] + view_logits[1]
    permuted = residue_permutation(chain_index, chain_swap)
    row_ids = (
        lax.axis_index("dap") * row_count
        + rep_index * half_rows
        + jnp.arange(half_rows, dtype=jnp.int32)
    )
    target = jnp.take(
        jnp.take(distance_bins, jnp.take(permuted, row_ids), axis=0), permuted, axis=1
    )
    log_total = jnp.log(jnp.sum(jnp.exp(logits), axis=-1, keepdims=True))
    bins = distogram_head.shape[1]
    onehot = (target[:, :, None] == jnp.arange(bins, dtype=jnp.int32)[None, None, :]).astype(
        jnp.float32
    )
    grad_logits = (jnp.exp(logits - log_total) - onehot).astype(jnp.bfloat16)
    d_head = jnp.einsum("srnc,rnb->cb", two_views, grad_logits, preferred_element_type=jnp.float32)
    grad_half = jnp.einsum(
        "rnb,cb->rnc", grad_logits, distogram_head, preferred_element_type=jnp.float32
    )
    grad_rows = lax.all_gather(grad_half.astype(jnp.bfloat16), "rep", axis=0, tiled=True).astype(
        grad_half.dtype
    )
    mirrored = jnp.swapaxes(
        lax.all_to_all(
            grad_rows.astype(jnp.bfloat16), "dap", split_axis=1, concat_axis=0, tiled=True
        ).astype(grad_rows.dtype),
        0,
        1,
    )
    grad_t = grad_rows + mirrored
    grad_mid_t, dw_in, dg_in, do_in = triangle_backward(
        grad_t, stored_in, incoming_weights, incoming_gate, incoming_output, (2, 3, 0, 1)
    )
    grad_mid = jnp.swapaxes(
        lax.all_to_all(
            grad_mid_t.astype(jnp.bfloat16), "dap", split_axis=1, concat_axis=0, tiled=True
        ).astype(grad_mid_t.dtype),
        0,
        1,
    )
    pair_grad, dw_out, dg_out, do_out = triangle_backward(
        grad_mid, stored_out, outgoing_weights, outgoing_gate, outgoing_output, (0, 1, 2, 3)
    )
    grad_sums = (
        lax.psum(dw_out.astype(jnp.bfloat16), "dap").astype(jnp.float32),
        lax.psum(dg_out.astype(jnp.bfloat16), "dap").astype(jnp.float32),
        lax.psum(do_out.astype(jnp.bfloat16), "dap").astype(jnp.float32),
        lax.psum(dw_in.astype(jnp.bfloat16), "dap").astype(jnp.float32),
        lax.psum(dg_in.astype(jnp.bfloat16), "dap").astype(jnp.float32),
        lax.psum(do_in.astype(jnp.bfloat16), "dap").astype(jnp.float32),
    )
    head_total = lax.psum(d_head, ("dap", "rep"))
    inv_count = 1.0 / residues
    return (
        pair_grad,
        grad_sums[0] * inv_count,
        grad_sums[1] * inv_count,
        grad_sums[2] * inv_count,
        grad_sums[3] * inv_count,
        grad_sums[4] * inv_count,
        grad_sums[5] * inv_count,
        head_total * inv_count,
    )


def gather_part(pair_input, matrices, dap, rep):
    rows, residues, channels = pair_input.shape
    half_rows = rows // rep
    rep_index = lax.axis_index("rep")
    dap_index = lax.axis_index("dap")
    own_rows = lax.dynamic_slice_in_dim(pair_input, rep_index * half_rows, half_rows, 0)
    stack = jnp.stack(matrices)
    count, depth, width = stack.shape
    share = depth // dap
    own_share = lax.dynamic_slice_in_dim(stack, dap_index * share, share, 1)
    pair_size = half_rows * residues * channels
    packed = jnp.concatenate(
        [own_rows.reshape(-1, channels), own_share.reshape(-1, channels)], axis=0
    )
    everything = lax.all_gather(packed, ("dap", "rep"), axis=0, tiled=False)
    split = pair_size // channels
    pair_all = everything[:, :split].reshape(dap * rows, residues, channels)
    tail = everything[:, split:].reshape(dap, rep, count, share, width)
    mats = jnp.transpose(tail, (2, 0, 3, 1, 4)).reshape(count, depth, rep * width)
    return (pair_all, mats)


F32, BF16 = jnp.float32, jnp.bfloat16
CH = 128
LANES = 128
GROUP = 2
UNROLL = 8


def dot(a, b, da=1, db=0):
    return lax.dot_general(a, b, (((da,), (db,)), ((), ())), preferred_element_type=F32)


def sigmoid(v):
    return 1.0 / (1.0 + jnp.exp(-v))


def mean0(v):
    return jnp.mean(v, axis=0, keepdims=True)


def norm0(v):
    centred = v - mean0(v)
    inverse = lax.rsqrt(mean0(centred * centred) + epsilon)
    return (centred * inverse, inverse)


def rounded(v):
    return v.astype(BF16).astype(F32)


def plane_load(ref, group, half, channels):
    tiles = [
        ref[pl.ds(group * GROUP + t, channels, stride=half), :] for t in range(GROUP)
    ]
    return jnp.concatenate(tiles, axis=1)


def plane_store(ref, group, half, values):
    for t in range(GROUP):
        ref[pl.ds(group * GROUP + t, values.shape[0], stride=half), :] = values[
            :, t * LANES : (t + 1) * LANES
        ]


def matrix_load(ref, channel, half):
    packed = ref[pl.ds(pl.multiple_of(channel * half, half), half), :]
    n = LANES // 2
    return jnp.concatenate([packed[:, :n], packed[:, n:]], axis=0)


def matrix_store(ref, channel, half, values):
    packed = jnp.concatenate([values[:half], values[half:]], axis=1)
    ref[pl.ds(pl.multiple_of(channel * half, half), half), :] = packed


def over(count, body):
    def step(index, carry):
        body(index)
        return carry

    lax.fori_loop(0, count, step, 0)


def over_channels(channels, body):
    def step(index):
        for u in range(UNROLL):
            body(index * UNROLL + u)

    over(channels // UNROLL, step)


def part_kernel(
    place,
    pair,
    mats,
    head,
    target,
    target_t,
    pair_grad,
    dw_out,
    dg_out,
    do_out,
    dw_in,
    dg_in,
    do_in,
    d_head,
    down,
    up,
    z0,
    z1,
    z2,
    go,
    p1,
    p2,
    y1,
    y2,
    a1,
    b1,
    x1,
    a2,
    b2,
    x2,
    lg,
    acc1,
    acc2,
    acc_o1,
    acc_o2,
    acc_h,
):
    n = pair.shape[0]
    half = n // 2
    groups = half // GROUP
    own_rows = pair_grad.shape[0]
    width = dg_out.shape[1]
    bins = head.shape[1]
    for side in range(2):
        for q in range(5):
            square = mats[side * 6 + q]
            up[side, :, q * CH : (q + 1) * CH] = square
            down[side, q * CH : (q + 1) * CH, :] = square.astype(F32).T.astype(BF16)
    out_t1, out_t2 = mats[5], mats[11]
    out_n1 = out_t1.astype(F32).T.astype(BF16)
    out_n2 = out_t2.astype(F32).T.astype(BF16)
    head_n = head[...]
    head_t = head_n.astype(F32).T.astype(BF16)
    heads = jnp.concatenate([head_n.astype(F32)] * 2, axis=1).astype(BF16)
    for ref in (acc1, acc2, acc_o1, acc_o2, acc_h):
        ref[...] = jnp.zeros_like(ref)

    def project(g, z, side, proj, a, b):
        hat, _ = norm0(z)
        p = dot(down[side], hat.astype(BF16))
        proj[g] = p
        plane_store(a, g, half, rounded(sigmoid(p[CH : 2 * CH]) * p[:CH]))
        plane_store(b, g, half, rounded(sigmoid(p[3 * CH : 4 * CH]) * p[2 * CH : 3 * CH]))

    def mix_norm(g, x):
        v = plane_load(x, g, half, CH)
        m = mean0(v)
        s = lax.rsqrt(mean0(v * v) - m * m + epsilon)
        return ((v - m) * s, s)

    def update(g, z, x, proj, y, out_t):
        hat, _ = mix_norm(g, x)
        upd = dot(out_t, hat.astype(BF16))
        y[g] = upd
        return rounded(z + sigmoid(proj[g, 4 * CH :, :]) * upd)

    def first(g):
        tiles = []
        for t in range(GROUP):
            row = g * GROUP + t
            cells = jnp.concatenate([pair[row].astype(F32), pair[row + half].astype(F32)], axis=0)
            tiles.append(cells.T)
        z = jnp.concatenate(tiles, axis=1)
        z0[g] = z
        project(g, z, 0, p1, a1, b1)

    over(groups, first)

    def mix_one(h):
        left = matrix_load(a1, h, half).astype(BF16)
        right = matrix_load(b1, h, half).astype(BF16)
        matrix_store(x1, h, half, dot(left, right, 1, 1))

    over_channels(CH, mix_one)

    def second(g):
        z = update(g, z0[g], x1, p1, y1, out_t1)
        z1[g] = z
        project(g, z, 1, p2, a2, b2)

    over(groups, second)

    def mix_two(h):
        left = matrix_load(a2, h, half).T.astype(BF16)
        right = matrix_load(b2, h, half).astype(BF16)
        matrix_store(x2, h, half, dot(left, right))

    over_channels(CH, mix_two)

    def third(g):
        z = update(g, z1[g], x2, p2, y2, out_t2).astype(BF16)
        z2[g] = z
        plane_store(lg, g, half, dot(head_t, z))

    over(groups, third)

    def mirror(b):
        v = matrix_load(lg, b, half)
        matrix_store(lg, b, half, v + v.T)

    over_channels(bins, mirror)

    def enter(g, grad, x, proj, y, out_n, acc_o):
        upd = y[g]
        gate = sigmoid(proj[g, 4 * CH :, :])
        scaled = grad * gate
        proj[g, 4 * CH :, :] = scaled * upd * (1.0 - gate)
        gy = scaled.astype(BF16)
        hat, s = mix_norm(g, x)
        acc_o[...] += dot(hat.astype(BF16), gy, 1, 1)
        gxn = dot(out_n, gy)
        gx = s * (gxn - mean0(gxn) - hat * mean0(gxn * hat))
        plane_store(x, g, half, rounded(gx))

    def loss(g):
        logits = plane_load(lg, g, half, bins)
        prob = jnp.exp(logits - jnp.log(jnp.sum(jnp.exp(logits), axis=0, keepdims=True)))
        ids = lax.broadcasted_iota(jnp.int32, logits.shape, 0)
        hot = (ids == target[g]).astype(F32)
        hot_t = (ids == target_t[g]).astype(F32)
        both = jnp.concatenate([prob - hot, prob - hot_t], axis=0).astype(BF16)
        grad = dot(heads, both)
        go[g] = grad
        acc_h[...] += dot(z2[g], both, 1, 1)
        enter(g, grad, x2, p2, y2, out_n2, acc_o2)

    over(groups, loss)

    def back_two(h):
        left = matrix_load(a2, h, half).astype(BF16)
        right = matrix_load(b2, h, half).astype(BF16)
        gx = matrix_load(x2, h, half).astype(BF16)
        matrix_store(a2, h, half, dot(right, gx, 1, 1))
        matrix_store(b2, h, half, dot(left, gx))

    over_channels(CH, back_two)

    def leave(g, z, proj, a, b, side, acc):
        ga = plane_load(a, g, half, CH)
        gb = plane_load(b, g, half, CH)
        sa = sigmoid(proj[g, CH : 2 * CH, :])
        sb = sigmoid(proj[g, 3 * CH : 4 * CH, :])
        ta, tb = ga * sa, gb * sb
        pieces = [
            ta,
            ta * proj[g, :CH, :] * (1.0 - sa),
            tb,
            tb * proj[g, 2 * CH : 3 * CH, :] * (1.0 - sb),
            proj[g, 4 * CH :, :],
        ]
        gp = jnp.concatenate([v.astype(BF16) for v in pieces], axis=0)
        hat, inverse = norm0(z)
        acc[...] += dot(gp, hat.astype(BF16), 1, 1)
        return (gp, hat, inverse)

    def finish(g, side, grad, gp, hat, inverse):
        gn = dot(up[side], gp)
        return grad + inverse * (gn - mean0(gn) - hat * mean0(gn * hat))

    def fourth(g):
        grad = finish(g, 1, go[g], *leave(g, z1[g], p2, a2, b2, 1, acc2))
        go[g] = grad
        enter(g, grad, x1, p1, y1, out_n1, acc_o1)

    over(groups, fourth)

    def back_one(h):
        left = matrix_load(a1, h, half).astype(BF16)
        right = matrix_load(b1, h, half).astype(BF16)
        gx = matrix_load(x1, h, half)
        matrix_store(a1, h, half, dot(gx.astype(BF16), right))
        matrix_store(b1, h, half, dot(gx.T.astype(BF16), left))

    over_channels(CH, back_one)

    row = place[0]
    upper = row // half
    low = row - upper * half
    n_lane = LANES // 2

    def last(g):
        gp, hat, inverse = leave(g, z0[g], p1, a1, b1, 0, acc1)

        @pl.when((g * GROUP >= low) & (g * GROUP < low + own_rows))
        def _():
            grad = finish(g, 0, go[g], gp, hat, inverse)
            for t in range(GROUP):
                cells = grad[:, t * LANES : (t + 1) * LANES].T
                chosen = jnp.where(upper == 0, cells[:n_lane], cells[n_lane:])
                pair_grad[g * GROUP + t - low] = chosen

    over(groups, last)

    scale = 1.0 / n
    start = pl.multiple_of(place[1], width)
    for acc, dw, dg in ((acc1, dw_out, dg_out), (acc2, dw_in, dg_in)):
        for q in range(4):
            dw[q] = acc[pl.ds(q * CH + start, width), :].T * scale
        dg[...] = acc[pl.ds(4 * CH + start, width), :].T * scale
    do_out[...] = acc_o1[pl.ds(start, width), :] * scale
    do_in[...] = acc_o2[pl.ds(start, width), :] * scale
    d_head[...] = (acc_h[:, :bins] + acc_h[:, bins:]) * scale


def whole_part(dap, rep):
    def run(
        pair_input,
        outgoing_weights,
        outgoing_gate,
        outgoing_output,
        incoming_weights,
        incoming_gate,
        incoming_output,
        distogram_head,
        distance_bins,
        chain_index,
        chain_swap,
    ):
        rows, n, _ = pair_input.shape
        bins = distogram_head.shape[1]
        width = outgoing_weights.shape[2]
        matrices = [outgoing_weights[q] for q in range(4)] + [outgoing_gate, outgoing_output.T]
        matrices += [incoming_weights[q] for q in range(4)] + [incoming_gate, incoming_output.T]
        pair_all, mats = gather_part(pair_input, matrices, dap, rep)
        permuted = residue_permutation(chain_index, chain_swap)
        positions = jnp.arange(n, dtype=jnp.int32)
        mover = (permuted[:, None] == positions[None, :]).astype(BF16)
        moved = jnp.einsum(
            "ia,ab,jb->ij", mover, distance_bins.astype(BF16), mover, preferred_element_type=F32
        ).astype(jnp.int32)
        groups = n // 2 // GROUP

        def blocks(values):
            split = values.reshape(2, groups, GROUP, n)
            return jnp.transpose(split, (1, 2, 0, 3)).reshape(groups, 1, GROUP * LANES)

        place = jnp.stack([lax.axis_index("dap") * rows, lax.axis_index("rep") * width])
        shape = jax.ShapeDtypeStruct
        vmem = pl.BlockSpec(memory_space=pltpu.VMEM)
        block = GROUP * LANES
        cells = pltpu.VMEM((groups, CH, block), F32)
        plane = pltpu.VMEM((CH * n // 2, LANES), F32)
        projected = pltpu.VMEM((groups, 5 * CH, block), F32)
        square = pltpu.VMEM((CH, CH), F32)
        return pl.pallas_call(
            part_kernel,
            out_shape=(
                shape((rows, n, CH), F32),
                shape((4, CH, width), F32),
                shape((CH, width), F32),
                shape((width, CH), F32),
                shape((4, CH, width), F32),
                shape((CH, width), F32),
                shape((width, CH), F32),
                shape((CH, bins), F32),
            ),
            in_specs=[pl.BlockSpec(memory_space=pltpu.SMEM)] + [vmem] * 5,
            out_specs=tuple([vmem] * 8),
            scratch_shapes=[
                pltpu.VMEM((2, 5 * CH, CH), BF16),
                pltpu.VMEM((2, CH, 5 * CH), BF16),
                cells,
                cells,
                pltpu.VMEM((groups, CH, block), BF16),
                cells,
                projected,
                projected,
                cells,
                cells,
                plane,
                plane,
                plane,
                plane,
                plane,
                plane,
                pltpu.VMEM((bins * n // 2, LANES), F32),
                pltpu.VMEM((5 * CH, CH), F32),
                pltpu.VMEM((5 * CH, CH), F32),
                square,
                square,
                square,
            ],
            compiler_params=pltpu.CompilerParams(vmem_limit_bytes=60 * 1024 * 1024),
        )(
            place.astype(jnp.int32),
            pair_all,
            mats,
            distogram_head,
            blocks(moved),
            blocks(moved.T),
        )

    return run


def solution(mesh):
    dap, rep = mesh.shape["dap"], mesh.shape["rep"]

    def plan(*arrays):
        residues, channels = arrays[0].shape[1], arrays[0].shape[2]
        width, bins = arrays[1].shape[2], arrays[7].shape[1]
        rows = arrays[0].shape[0]
        small = residues == LANES // 2 and channels == CH and width * rep == CH
        small = small and bins * 2 == CH and rows % rep == 0 and rows % GROUP == 0
        small = small and (residues // 2) % rows == 0 and channels % dap == 0
        return (whole_part(dap, rep) if small else per_device)(*arrays)

    return jax.shard_map(
        plan,
        mesh=mesh,
        in_specs=(
            P(("groups", "dap"), None, None),
            P(None, None, "rep"),
            P(None, "rep"),
            P("rep", None),
            P(None, None, "rep"),
            P(None, "rep"),
            P("rep", None),
            P(),
            P("groups", None),
            P("groups"),
            P("groups"),
        ),
        out_specs=(
            P(("groups", "dap"), None, None),
            P("groups", None, "rep"),
            P("groups", "rep"),
            P(("groups", "rep"), None),
            P("groups", None, "rep"),
            P("groups", "rep"),
            P(("groups", "rep"), None),
            P("groups", None),
        ),
        check_vma=False,
    )
```

```python
import functools

import jax
import jax.numpy as jnp
from jax import lax
from jax.experimental import pallas as pl
from jax.experimental.pallas import tpu as pltpu
from jax.sharding import PartitionSpec as P

H = 128


epsilon = 1e-05


def normalize(values):
    center = jnp.mean(values, axis=-1, keepdims=True)
    centred = values - center
    inverse = lax.rsqrt(jnp.mean(centred * centred, axis=-1, keepdims=True) + epsilon)
    return (centred * inverse, inverse)


def triangle_forward(pair_rows, weights, gate_w, out_w, roles):
    value_left, gate_left, value_right, gate_right = roles
    pair_float = pair_rows.astype(jnp.float32)
    pair_hat, pair_inverse = normalize(pair_float)
    normed = pair_hat.astype(jnp.bfloat16)
    projected = jnp.einsum("rnc,qch->qhrn", normed, weights, preferred_element_type=jnp.float32)
    local_side = (jax.nn.sigmoid(projected[gate_left]) * projected[value_left]).astype(jnp.bfloat16)
    remote_side = (jax.nn.sigmoid(projected[gate_right]) * projected[value_right]).astype(
        jnp.bfloat16
    )
    remote_all = lax.all_gather(remote_side, "dap", axis=1, tiled=True)
    mixed_sum = jnp.einsum(
        "hik,hjk->hij", local_side, remote_all, preferred_element_type=jnp.float32
    )
    total_one, total_two = lax.psum(
        (jnp.sum(mixed_sum, axis=0), jnp.sum(mixed_sum * mixed_sum, axis=0)), "rep"
    )
    mean_hidden = total_one / H
    inv_hidden = lax.rsqrt(total_two / H - mean_hidden * mean_hidden + epsilon)
    mixed_hat = (mixed_sum - mean_hidden) * inv_hidden
    mixed_norm = mixed_hat.astype(jnp.bfloat16)
    partial_out = jnp.einsum("hrn,hc->rnc", mixed_norm, out_w, preferred_element_type=jnp.float32)
    update_half = lax.psum_scatter(partial_out, "rep", scatter_dimension=2, tiled=True)
    gating = jax.nn.sigmoid(
        jnp.einsum("rnc,cd->rnd", normed, gate_w, preferred_element_type=jnp.float32)
    )
    update_full = lax.all_gather(gating * update_half, "rep", axis=2, tiled=True)
    result = (pair_float + update_full).astype(jnp.bfloat16)
    stored = (
        pair_hat,
        pair_inverse,
        normed,
        projected,
        local_side,
        remote_all,
        mixed_hat,
        inv_hidden,
        mixed_norm,
        update_half,
        gating,
    )
    return (result, stored)


def triangle_backward(grad_out, stored, weights, gate_w, out_w, roles):
    (
        pair_hat,
        pair_inverse,
        normed,
        projected,
        local_side,
        carried,
        mixed_hat,
        inv_hidden,
        mixed_norm,
        update_half,
        gating,
    ) = stored
    value_left, gate_left, value_right, gate_right = roles
    width_half = gate_w.shape[1]
    rep_index = lax.axis_index("rep")
    grad_half = lax.dynamic_slice_in_dim(grad_out, rep_index * width_half, width_half, 2)
    grad_gate = (grad_half * update_half * gating * (1.0 - gating)).astype(jnp.bfloat16)
    update_grad_half = (grad_half * gating).astype(jnp.bfloat16)
    grad_update = lax.all_gather(update_grad_half, "rep", axis=2, tiled=True)
    d_gate = jnp.einsum("rnc,rnd->cd", normed, grad_gate, preferred_element_type=jnp.float32)
    d_output = jnp.einsum(
        "hrn,rnc->hc", mixed_norm, grad_update, preferred_element_type=jnp.float32
    )
    grad_norm = jnp.einsum("rnc,hc->hrn", grad_update, out_w, preferred_element_type=jnp.float32)
    sum_one, sum_two = lax.psum(
        (jnp.sum(grad_norm, axis=0), jnp.sum(grad_norm * mixed_hat, axis=0)), "rep"
    )
    grad_mixed = (inv_hidden * (grad_norm - sum_one / H - mixed_hat * (sum_two / H))).astype(
        jnp.bfloat16
    )
    grad_local = jnp.einsum("hij,hjk->hik", grad_mixed, carried, preferred_element_type=jnp.float32)
    swapped = lax.psum_scatter(
        jnp.einsum(
            "hij,hik->jhk", grad_mixed, local_side, preferred_element_type=jnp.float32
        ).astype(jnp.bfloat16),
        "dap",
        scatter_dimension=0,
        tiled=True,
    ).astype(jnp.float32)
    grad_remote = jnp.swapaxes(swapped, 0, 1)
    sigmoid_left = jax.nn.sigmoid(projected[gate_left])
    sigmoid_right = jax.nn.sigmoid(projected[gate_right])
    pieces = [None, None, None, None]
    pieces[value_left] = grad_local * sigmoid_left
    pieces[gate_left] = grad_local * projected[value_left] * sigmoid_left * (1.0 - sigmoid_left)
    pieces[value_right] = grad_remote * sigmoid_right
    pieces[gate_right] = (
        grad_remote * projected[value_right] * sigmoid_right * (1.0 - sigmoid_right)
    )
    grad_proj = jnp.stack(pieces).astype(jnp.bfloat16)
    d_weights = jnp.einsum("rnc,qhrn->qch", normed, grad_proj, preferred_element_type=jnp.float32)
    partial_sum = jnp.einsum(
        "qhrn,qch->rnc", grad_proj, weights, preferred_element_type=jnp.float32
    )
    partial_sum = partial_sum + jnp.einsum(
        "rnd,cd->rnc", grad_gate, gate_w, preferred_element_type=jnp.float32
    )
    grad_normed = lax.psum(partial_sum.astype(jnp.bfloat16), "rep").astype(jnp.float32)
    grad_in = grad_out + pair_inverse * (
        grad_normed
        - jnp.mean(grad_normed, axis=-1, keepdims=True)
        - pair_hat * jnp.mean(grad_normed * pair_hat, axis=-1, keepdims=True)
    )
    return (grad_in, d_weights, d_gate, d_output)


def residue_permutation(chain_index, chain_swap):
    chains = chain_swap.shape[0]
    chain_ids = jnp.arange(chains, dtype=jnp.int32)
    starts = jnp.sum((chain_index[None, :] < chain_ids[:, None]).astype(jnp.int32), axis=1)
    mapped_starts = jnp.sum(
        (chain_swap[:, None] == chain_ids[None, :]).astype(jnp.int32) * starts[None, :], axis=1
    )
    member = (chain_index[:, None] == chain_ids[None, :]).astype(jnp.int32)
    own_start = jnp.sum(member * starts[None, :], axis=1)
    new_start = jnp.sum(member * mapped_starts[None, :], axis=1)
    positions = jnp.arange(chain_index.shape[0], dtype=jnp.int32)
    return positions - own_start + new_start


def per_device(
    pair_input,
    outgoing_weights,
    outgoing_gate,
    outgoing_output,
    incoming_weights,
    incoming_gate,
    incoming_output,
    distogram_head,
    distance_bins,
    chain_index,
    chain_swap,
):
    row_count = pair_input.shape[0]
    residues = pair_input.shape[1]
    middle, stored_out = triangle_forward(
        pair_input, outgoing_weights, outgoing_gate, outgoing_output, (0, 1, 2, 3)
    )
    middle_t = jnp.swapaxes(
        lax.all_to_all(middle, "dap", split_axis=1, concat_axis=0, tiled=True), 0, 1
    )
    final_t, stored_in = triangle_forward(
        middle_t, incoming_weights, incoming_gate, incoming_output, (2, 3, 0, 1)
    )
    final_rows = jnp.swapaxes(
        lax.all_to_all(final_t, "dap", split_axis=1, concat_axis=0, tiled=True), 0, 1
    )
    half_rows = row_count // lax.axis_size("rep")
    rep_index = lax.axis_index("rep")
    own_rows = lax.dynamic_slice_in_dim(final_rows, rep_index * half_rows, half_rows, 0)
    own_cols = lax.dynamic_slice_in_dim(final_t, rep_index * half_rows, half_rows, 0)
    two_views = jnp.stack([own_rows, own_cols])
    view_logits = jnp.einsum(
        "srnc,cb->srnb", two_views, distogram_head, preferred_element_type=jnp.float32
    )
    logits = view_logits[0] + view_logits[1]
    permuted = residue_permutation(chain_index, chain_swap)
    row_ids = (
        lax.axis_index("dap") * row_count
        + rep_index * half_rows
        + jnp.arange(half_rows, dtype=jnp.int32)
    )
    target = jnp.take(
        jnp.take(distance_bins, jnp.take(permuted, row_ids), axis=0), permuted, axis=1
    )
    log_total = jnp.log(jnp.sum(jnp.exp(logits), axis=-1, keepdims=True))
    bins = distogram_head.shape[1]
    onehot = (target[:, :, None] == jnp.arange(bins, dtype=jnp.int32)[None, None, :]).astype(
        jnp.float32
    )
    grad_logits = (jnp.exp(logits - log_total) - onehot).astype(jnp.bfloat16)
    d_head = jnp.einsum("srnc,rnb->cb", two_views, grad_logits, preferred_element_type=jnp.float32)
    grad_half = jnp.einsum(
        "rnb,cb->rnc", grad_logits, distogram_head, preferred_element_type=jnp.float32
    )
    grad_rows = lax.all_gather(grad_half.astype(jnp.bfloat16), "rep", axis=0, tiled=True).astype(
        grad_half.dtype
    )
    mirrored = jnp.swapaxes(
        lax.all_to_all(
            grad_rows.astype(jnp.bfloat16), "dap", split_axis=1, concat_axis=0, tiled=True
        ).astype(grad_rows.dtype),
        0,
        1,
    )
    grad_t = grad_rows + mirrored
    grad_mid_t, dw_in, dg_in, do_in = triangle_backward(
        grad_t, stored_in, incoming_weights, incoming_gate, incoming_output, (2, 3, 0, 1)
    )
    grad_mid = jnp.swapaxes(
        lax.all_to_all(
            grad_mid_t.astype(jnp.bfloat16), "dap", split_axis=1, concat_axis=0, tiled=True
        ).astype(grad_mid_t.dtype),
        0,
        1,
    )
    pair_grad, dw_out, dg_out, do_out = triangle_backward(
        grad_mid, stored_out, outgoing_weights, outgoing_gate, outgoing_output, (0, 1, 2, 3)
    )
    grad_sums = (
        lax.psum(dw_out.astype(jnp.bfloat16), "dap").astype(jnp.float32),
        lax.psum(dg_out.astype(jnp.bfloat16), "dap").astype(jnp.float32),
        lax.psum(do_out.astype(jnp.bfloat16), "dap").astype(jnp.float32),
        lax.psum(dw_in.astype(jnp.bfloat16), "dap").astype(jnp.float32),
        lax.psum(dg_in.astype(jnp.bfloat16), "dap").astype(jnp.float32),
        lax.psum(do_in.astype(jnp.bfloat16), "dap").astype(jnp.float32),
    )
    head_total = lax.psum(d_head, ("dap", "rep"))
    inv_count = 1.0 / residues
    return (
        pair_grad,
        grad_sums[0] * inv_count,
        grad_sums[1] * inv_count,
        grad_sums[2] * inv_count,
        grad_sums[3] * inv_count,
        grad_sums[4] * inv_count,
        grad_sums[5] * inv_count,
        head_total * inv_count,
    )


F32, BF16 = jnp.float32, jnp.bfloat16
CH = 128
LANES = 128
GROUP = 2
UNROLL = 8


def dot(a, b, da=1, db=0):
    return lax.dot_general(a, b, (((da,), (db,)), ((), ())), preferred_element_type=F32)


def sigmoid(v):
    return 0.5 * jnp.tanh(0.5 * v) + 0.5


def mean0(v):
    return jnp.mean(v, axis=0, keepdims=True)


def norm0(v):
    centred = v - mean0(v)
    inverse = lax.rsqrt(mean0(centred * centred) + epsilon)
    return (centred * inverse, inverse)


def rounded(v):
    return v.astype(BF16).astype(F32)


def plane_load(ref, group, half, channels):
    tiles = [
        ref[pl.ds(group * GROUP + t, channels, stride=half), :] for t in range(GROUP)
    ]
    return jnp.concatenate(tiles, axis=1)


def plane_store(ref, group, half, values):
    for t in range(GROUP):
        ref[pl.ds(group * GROUP + t, values.shape[0], stride=half), :] = values[
            :, t * LANES : (t + 1) * LANES
        ]


def matrix_load(ref, channel, half):
    packed = ref[pl.ds(pl.multiple_of(channel * half, half), half), :]
    n = LANES // 2
    return jnp.concatenate([packed[:, :n], packed[:, n:]], axis=0)


def matrix_store(ref, channel, half, values):
    packed = jnp.concatenate([values[:half], values[half:]], axis=1)
    ref[pl.ds(pl.multiple_of(channel * half, half), half), :] = packed


def over(count, body):
    def step(index, carry):
        body(index)
        return carry

    lax.fori_loop(0, count, step, 0)


def over_channels(channels, body):
    def step(index):
        for u in range(UNROLL):
            body(index * UNROLL + u)

    over(channels // UNROLL, step)


def part_kernel(
    place,
    pair,
    mats,
    head,
    target,
    pair_grad,
    dw_out,
    dg_out,
    do_out,
    dw_in,
    dg_in,
    do_in,
    d_head,
    down,
    up,
    z0,
    z1,
    z2,
    go,
    p1,
    p2,
    y1,
    y2,
    a1,
    b1,
    x1,
    a2,
    b2,
    x2,
    lg,
    acc1,
    acc2,
    acc_o1,
    acc_o2,
    acc_h,
    target_t,
):
    n = pair.shape[0]
    half = n // 2
    groups = half // GROUP
    own_rows = pair_grad.shape[0]
    width = dg_out.shape[0]
    bins = head.shape[0]
    def square(index):
        return jnp.concatenate([mats[0, index], mats[1, index]], axis=0)

    def turned(values):
        return values.astype(F32).T.astype(BF16)

    for side in range(2):
        for q in range(5):
            matrix = square(side * 6 + q)
            down[side, q * CH : (q + 1) * CH, :] = matrix
            up[side, :, q * CH : (q + 1) * CH] = turned(matrix)
    out_n1, out_n2 = square(5), square(11)
    out_t1, out_t2 = turned(out_n1), turned(out_n2)
    head_t = head[...]
    heads = turned(jnp.concatenate([head_t, head_t], axis=0))
    target_t[...] = target[...].T
    for ref in (acc1, acc2, acc_o1, acc_o2, acc_h):
        ref[...] = jnp.zeros_like(ref)

    def project(g, z, side, proj, a, b):
        hat, _ = norm0(z)
        p = dot(down[side], hat.astype(BF16))
        proj[g] = p
        plane_store(a, g, half, rounded(sigmoid(p[CH : 2 * CH]) * p[:CH]))
        plane_store(b, g, half, rounded(sigmoid(p[3 * CH : 4 * CH]) * p[2 * CH : 3 * CH]))

    def mix_norm(g, x):
        v = plane_load(x, g, half, CH)
        m = mean0(v)
        s = lax.rsqrt(mean0(v * v) - m * m + epsilon)
        return ((v - m) * s, s)

    def update(g, z, x, proj, y, out_t):
        hat, _ = mix_norm(g, x)
        upd = dot(out_t, hat.astype(BF16))
        y[g] = upd
        return rounded(z + sigmoid(proj[g, 4 * CH :, :]) * upd)

    def first(g):
        tiles = []
        for t in range(GROUP):
            row = g * GROUP + t
            cells = jnp.concatenate([pair[row].astype(F32), pair[row + half].astype(F32)], axis=0)
            tiles.append(cells.T)
        z = jnp.concatenate(tiles, axis=1)
        z0[g] = z
        project(g, z, 0, p1, a1, b1)

    over(groups, first)

    def mix_one(h):
        left = matrix_load(a1, h, half).astype(BF16)
        right = matrix_load(b1, h, half).astype(BF16)
        matrix_store(x1, h, half, dot(left, right, 1, 1))

    over_channels(CH, mix_one)

    def second(g):
        z = update(g, z0[g], x1, p1, y1, out_t1)
        z1[g] = z
        project(g, z, 1, p2, a2, b2)

    over(groups, second)

    def mix_two(h):
        left = matrix_load(a2, h, half).T.astype(BF16)
        right = matrix_load(b2, h, half).astype(BF16)
        matrix_store(x2, h, half, dot(left, right))

    over_channels(CH, mix_two)

    def third(g):
        z = update(g, z1[g], x2, p2, y2, out_t2).astype(BF16)
        z2[g] = z
        plane_store(lg, g, half, dot(head_t, z))

    over(groups, third)

    def mirror(b):
        v = matrix_load(lg, b, half)
        matrix_store(lg, b, half, v + v.T)

    over_channels(bins, mirror)

    def enter(g, grad, x, proj, y, out_n, acc_o):
        upd = y[g]
        gate = sigmoid(proj[g, 4 * CH :, :])
        scaled = grad * gate
        proj[g, 4 * CH :, :] = scaled * upd * (1.0 - gate)
        gy = scaled.astype(BF16)
        hat, s = mix_norm(g, x)
        acc_o[...] += dot(hat.astype(BF16), gy, 1, 1)
        gxn = dot(out_n, gy)
        gx = s * (gxn - mean0(gxn) - hat * mean0(gxn * hat))
        plane_store(x, g, half, rounded(gx))

    def lane_row(ref, g):
        rows = [g * GROUP + t + upper * half for t in range(GROUP) for upper in range(2)]
        return jnp.concatenate([ref[pl.ds(row, 1), :] for row in rows], axis=1)

    def loss(g):
        logits = plane_load(lg, g, half, bins)
        prob = jnp.exp(logits - jnp.log(jnp.sum(jnp.exp(logits), axis=0, keepdims=True)))
        ids = lax.broadcasted_iota(jnp.int32, logits.shape, 0).astype(F32)
        hot = (ids == lane_row(target, g)).astype(F32)
        hot_t = (ids == lane_row(target_t, g)).astype(F32)
        both = jnp.concatenate([prob - hot, prob - hot_t], axis=0).astype(BF16)
        grad = dot(heads, both)
        go[g] = grad
        acc_h[...] += dot(both, z2[g], 1, 1)
        enter(g, grad, x2, p2, y2, out_n2, acc_o2)

    over(groups, loss)

    def back_two(h):
        left = matrix_load(a2, h, half).astype(BF16)
        right = matrix_load(b2, h, half).astype(BF16)
        gx = matrix_load(x2, h, half).astype(BF16)
        matrix_store(a2, h, half, dot(right, gx, 1, 1))
        matrix_store(b2, h, half, dot(left, gx))

    over_channels(CH, back_two)

    def leave(g, z, proj, a, b, side, acc):
        ga = plane_load(a, g, half, CH)
        gb = plane_load(b, g, half, CH)
        sa = sigmoid(proj[g, CH : 2 * CH, :])
        sb = sigmoid(proj[g, 3 * CH : 4 * CH, :])
        ta, tb = ga * sa, gb * sb
        pieces = [
            ta,
            ta * proj[g, :CH, :] * (1.0 - sa),
            tb,
            tb * proj[g, 2 * CH : 3 * CH, :] * (1.0 - sb),
            proj[g, 4 * CH :, :],
        ]
        gp = jnp.concatenate([v.astype(BF16) for v in pieces], axis=0)
        hat, inverse = norm0(z)
        acc[...] += dot(gp, hat.astype(BF16), 1, 1)
        return (gp, hat, inverse)

    def finish(g, side, grad, gp, hat, inverse):
        gn = dot(up[side], gp)
        return grad + inverse * (gn - mean0(gn) - hat * mean0(gn * hat))

    def fourth(g):
        grad = finish(g, 1, go[g], *leave(g, z1[g], p2, a2, b2, 1, acc2))
        go[g] = grad
        enter(g, grad, x1, p1, y1, out_n1, acc_o1)

    over(groups, fourth)

    def back_one(h):
        left = matrix_load(a1, h, half).astype(BF16)
        right = matrix_load(b1, h, half).astype(BF16)
        gx = matrix_load(x1, h, half)
        matrix_store(a1, h, half, dot(gx.astype(BF16), right))
        matrix_store(b1, h, half, dot(gx.T.astype(BF16), left))

    over_channels(CH, back_one)

    row = place[0]
    upper = row // half
    low = row - upper * half
    n_lane = LANES // 2

    def last(g):
        gp, hat, inverse = leave(g, z0[g], p1, a1, b1, 0, acc1)

        @pl.when((g * GROUP >= low) & (g * GROUP < low + own_rows))
        def _():
            grad = finish(g, 0, go[g], gp, hat, inverse)
            for t in range(GROUP):
                cells = grad[:, t * LANES : (t + 1) * LANES].T
                chosen = jnp.where(upper == 0, cells[:n_lane], cells[n_lane:])
                pair_grad[g * GROUP + t - low] = chosen

    over(groups, last)

    scale = 1.0 / n
    start = pl.multiple_of(place[1], width)
    for acc, dw, dg in ((acc1, dw_out, dg_out), (acc2, dw_in, dg_in)):
        for q in range(4):
            dw[q] = acc[pl.ds(q * CH + start, width), :] * scale
        dg[...] = acc[pl.ds(4 * CH + start, width), :] * scale
    do_out[...] = acc_o1[pl.ds(start, width), :] * scale
    do_in[...] = acc_o2[pl.ds(start, width), :] * scale
    d_head[...] = (acc_h[:bins] + acc_h[bins:]) * scale


def gather_kernel(
    dap,
    pair,
    w_out,
    g_out,
    o_out,
    w_in,
    g_in,
    o_in,
    pair_all,
    mats,
    send_sem,
    recv_sem,
    send_mats,
    recv_mats,
):
    fars = dap // 2
    mine, rep = lax.axis_index("dap"), lax.axis_index("rep")
    far, near = mine // 2, mine % 2
    size = pair_all.shape[1]

    def origin(step):
        return lax.rem(far - step + fars, fars)

    def slot(origin_far, origin_near, origin_rep):
        return (origin_far * 2 + origin_near) * 2 + origin_rep

    along = [{"dap": lax.rem(far + step, fars) * 2 + near, "rep": rep} for step in range(fars)]
    across = {"dap": far * 2 + 1 - near, "rep": rep}
    partner = {"dap": mine, "rep": 1 - rep}

    barrier = pltpu.get_barrier_semaphore()
    peers = along[1:] + [across, partner]
    for peer in peers:
        pl.semaphore_signal(barrier, inc=1, device_id=peer, device_id_type=pl.DeviceIdType.MESH)

    own = slot(far, near, rep)
    pair_all[own] = pair[pl.ds(pl.multiple_of(rep * size, size), size), :]
    mats[rep, 0:4] = w_out[...]
    mats[rep, 4] = g_out[...]
    mats[rep, 5] = o_out[...]
    mats[rep, 6:10] = w_in[...]
    mats[rep, 10] = g_in[...]
    mats[rep, 11] = o_in[...]
    pl.semaphore_wait(barrier, len(peers))

    started = []

    def send(place, index, device):
        copy = pltpu.make_async_remote_copy(
            src_ref=pair_all.at[place],
            dst_ref=pair_all.at[place],
            send_sem=send_sem.at[index],
            recv_sem=recv_sem.at[index],
            device_id=device,
            device_id_type=pl.DeviceIdType.MESH,
        )
        copy.start()
        started.append(copy)

    def await_block(place, index, device):
        pltpu.make_async_remote_copy(
            src_ref=pair_all.at[place],
            dst_ref=pair_all.at[place],
            send_sem=send_sem.at[index],
            recv_sem=recv_sem.at[index],
            device_id=device,
            device_id_type=pl.DeviceIdType.MESH,
        ).wait_recv()

    near_base = fars
    rep_base = 2 * fars
    for step in range(1, fars):
        send(own, step, along[step])
    send(own, near_base, across)
    copy_mats = pltpu.make_async_remote_copy(
        src_ref=mats.at[rep],
        dst_ref=mats.at[rep],
        send_sem=send_mats,
        recv_sem=recv_mats,
        device_id=partner,
        device_id_type=pl.DeviceIdType.MESH,
    )
    copy_mats.start()
    send(own, rep_base, partner)
    for step in range(1, fars):
        place = slot(origin(step), near, rep)
        await_block(place, step, along[step])
        send(place, near_base + step, across)
        send(place, rep_base + step, partner)
    for step in range(fars):
        place = slot(origin(step), 1 - near, rep)
        await_block(place, near_base + step, across)
        send(place, rep_base + fars + step, partner)
    for step in range(fars):
        await_block(slot(origin(step), near, 1 - rep), rep_base + step, partner)
        await_block(slot(origin(step), 1 - near, 1 - rep), rep_base + fars + step, partner)
    copy_mats.wait_recv()
    for copy in started:
        copy.wait_send()
    copy_mats.wait_send()


def gather_part(dap, pair, *matrices):
    size = pair.shape[0] // 2
    width = matrices[2].shape[0]
    fars = dap // 2
    vmem = pl.BlockSpec(memory_space=pltpu.VMEM)
    return pl.pallas_call(
        functools.partial(gather_kernel, dap),
        out_shape=(
            jax.ShapeDtypeStruct((dap * 2, size, CH), BF16),
            jax.ShapeDtypeStruct((2, 12, width, CH), BF16),
        ),
        in_specs=[vmem] * 7,
        out_specs=(vmem, vmem),
        scratch_shapes=[
            pltpu.SemaphoreType.DMA((4 * fars,)),
            pltpu.SemaphoreType.DMA((4 * fars,)),
            pltpu.SemaphoreType.DMA,
            pltpu.SemaphoreType.DMA,
        ],
        compiler_params=pltpu.CompilerParams(
            collective_id=0, has_side_effects=True, vmem_limit_bytes=32 * 1024 * 1024
        ),
    )(pair, *matrices)


def whole_part(dap, rep):
    def run(
        pair_input,
        outgoing_weights,
        outgoing_gate,
        outgoing_output,
        incoming_weights,
        incoming_gate,
        incoming_output,
        distogram_head,
        distance_bins,
        chain_index,
        chain_swap,
    ):
        rows, n, _ = pair_input.shape
        bins = distogram_head.shape[1]
        width = outgoing_weights.shape[2]
        pair_all, mats = gather_part(
            dap,
            pair_input.reshape(rows * n, CH),
            jnp.swapaxes(outgoing_weights, 1, 2),
            outgoing_gate.T,
            outgoing_output,
            jnp.swapaxes(incoming_weights, 1, 2),
            incoming_gate.T,
            incoming_output,
        )
        permuted = residue_permutation(chain_index, chain_swap)
        positions = jnp.arange(n, dtype=jnp.int32)
        mover = (permuted[:, None] == positions[None, :]).astype(BF16)
        moved = jnp.einsum(
            "ia,ab,jb->ij", mover, distance_bins.astype(BF16), mover, preferred_element_type=F32
        )
        groups = n // 2 // GROUP

        place = jnp.stack([lax.axis_index("dap") * rows, lax.axis_index("rep") * width])
        shape = jax.ShapeDtypeStruct
        vmem = pl.BlockSpec(memory_space=pltpu.VMEM)
        block = GROUP * LANES
        cells = pltpu.VMEM((groups, CH, block), F32)
        plane = pltpu.VMEM((CH * n // 2, LANES), F32)
        projected = pltpu.VMEM((groups, 5 * CH, block), F32)
        square = pltpu.VMEM((CH, CH), F32)
        outs = pl.pallas_call(
            part_kernel,
            out_shape=(
                shape((rows, n, CH), F32),
                shape((4, width, CH), F32),
                shape((width, CH), F32),
                shape((width, CH), F32),
                shape((4, width, CH), F32),
                shape((width, CH), F32),
                shape((width, CH), F32),
                shape((bins, CH), F32),
            ),
            in_specs=[pl.BlockSpec(memory_space=pltpu.SMEM)] + [vmem] * 4,
            out_specs=tuple([vmem] * 8),
            scratch_shapes=[
                pltpu.VMEM((2, 5 * CH, CH), BF16),
                pltpu.VMEM((2, CH, 5 * CH), BF16),
                cells,
                cells,
                pltpu.VMEM((groups, CH, block), BF16),
                cells,
                projected,
                projected,
                cells,
                cells,
                plane,
                plane,
                plane,
                plane,
                plane,
                plane,
                pltpu.VMEM((bins * n // 2, LANES), F32),
                pltpu.VMEM((5 * CH, CH), F32),
                pltpu.VMEM((5 * CH, CH), F32),
                square,
                square,
                square,
                pltpu.VMEM((n, n), F32),
            ],
            compiler_params=pltpu.CompilerParams(vmem_limit_bytes=60 * 1024 * 1024),
        )(
            place.astype(jnp.int32),
            pair_all.reshape(dap * rows, n, CH),
            mats,
            distogram_head.T,
            moved,
        )
        pair_grad, dw_out, dg_out, do_out, dw_in, dg_in, do_in, d_head = outs
        return (
            pair_grad,
            jnp.swapaxes(dw_out, 1, 2),
            dg_out.T,
            do_out,
            jnp.swapaxes(dw_in, 1, 2),
            dg_in.T,
            do_in,
            d_head.T,
        )

    return run


def solution(mesh):
    dap, rep = mesh.shape["dap"], mesh.shape["rep"]

    def plan(*arrays):
        residues, channels = arrays[0].shape[1], arrays[0].shape[2]
        width, bins = arrays[1].shape[2], arrays[7].shape[1]
        rows = arrays[0].shape[0]
        small = residues == LANES // 2 and channels == CH and width * rep == CH
        small = small and bins * 2 == CH and rep == 2 and dap % 2 == 0 and rows % 2 == 0 and rows % GROUP == 0
        small = small and (residues // 2) % rows == 0
        return (whole_part(dap, rep) if small else per_device)(*arrays)

    return jax.shard_map(
        plan,
        mesh=mesh,
        in_specs=(
            P(("groups", "dap"), None, None),
            P(None, None, "rep"),
            P(None, "rep"),
            P("rep", None),
            P(None, None, "rep"),
            P(None, "rep"),
            P("rep", None),
            P(),
            P("groups", None),
            P("groups"),
            P("groups"),
        ),
        out_specs=(
            P(("groups", "dap"), None, None),
            P("groups", None, "rep"),
            P("groups", "rep"),
            P(("groups", "rep"), None),
            P("groups", None, "rep"),
            P("groups", "rep"),
            P(("groups", "rep"), None),
            P("groups", None),
        ),
        check_vma=False,
    )
```

```python
import functools

import jax
import jax.numpy as jnp
from jax import lax
from jax.experimental import pallas as pl
from jax.experimental.pallas import tpu as pltpu
from jax.sharding import PartitionSpec as P

H = 128


epsilon = 1e-05


def normalize(values):
    center = jnp.mean(values, axis=-1, keepdims=True)
    centred = values - center
    inverse = lax.rsqrt(jnp.mean(centred * centred, axis=-1, keepdims=True) + epsilon)
    return (centred * inverse, inverse)


def triangle_forward(pair_rows, weights, gate_w, out_w, roles):
    value_left, gate_left, value_right, gate_right = roles
    pair_float = pair_rows.astype(jnp.float32)
    pair_hat, pair_inverse = normalize(pair_float)
    normed = pair_hat.astype(jnp.bfloat16)
    projected = jnp.einsum("rnc,qch->qhrn", normed, weights, preferred_element_type=jnp.float32)
    local_side = (jax.nn.sigmoid(projected[gate_left]) * projected[value_left]).astype(jnp.bfloat16)
    remote_side = (jax.nn.sigmoid(projected[gate_right]) * projected[value_right]).astype(
        jnp.bfloat16
    )
    remote_all = lax.all_gather(remote_side, "dap", axis=1, tiled=True)
    mixed_sum = jnp.einsum(
        "hik,hjk->hij", local_side, remote_all, preferred_element_type=jnp.float32
    )
    total_one, total_two = lax.psum(
        (jnp.sum(mixed_sum, axis=0), jnp.sum(mixed_sum * mixed_sum, axis=0)), "rep"
    )
    mean_hidden = total_one / H
    inv_hidden = lax.rsqrt(total_two / H - mean_hidden * mean_hidden + epsilon)
    mixed_hat = (mixed_sum - mean_hidden) * inv_hidden
    mixed_norm = mixed_hat.astype(jnp.bfloat16)
    partial_out = jnp.einsum("hrn,hc->rnc", mixed_norm, out_w, preferred_element_type=jnp.float32)
    update_half = lax.psum_scatter(partial_out, "rep", scatter_dimension=2, tiled=True)
    gating = jax.nn.sigmoid(
        jnp.einsum("rnc,cd->rnd", normed, gate_w, preferred_element_type=jnp.float32)
    )
    update_full = lax.all_gather(gating * update_half, "rep", axis=2, tiled=True)
    result = (pair_float + update_full).astype(jnp.bfloat16)
    stored = (
        pair_hat,
        pair_inverse,
        normed,
        projected,
        local_side,
        remote_all,
        mixed_hat,
        inv_hidden,
        mixed_norm,
        update_half,
        gating,
    )
    return (result, stored)


def triangle_backward(grad_out, stored, weights, gate_w, out_w, roles):
    (
        pair_hat,
        pair_inverse,
        normed,
        projected,
        local_side,
        carried,
        mixed_hat,
        inv_hidden,
        mixed_norm,
        update_half,
        gating,
    ) = stored
    value_left, gate_left, value_right, gate_right = roles
    width_half = gate_w.shape[1]
    rep_index = lax.axis_index("rep")
    grad_half = lax.dynamic_slice_in_dim(grad_out, rep_index * width_half, width_half, 2)
    grad_gate = (grad_half * update_half * gating * (1.0 - gating)).astype(jnp.bfloat16)
    update_grad_half = (grad_half * gating).astype(jnp.bfloat16)
    grad_update = lax.all_gather(update_grad_half, "rep", axis=2, tiled=True)
    d_gate = jnp.einsum("rnc,rnd->cd", normed, grad_gate, preferred_element_type=jnp.float32)
    d_output = jnp.einsum(
        "hrn,rnc->hc", mixed_norm, grad_update, preferred_element_type=jnp.float32
    )
    grad_norm = jnp.einsum("rnc,hc->hrn", grad_update, out_w, preferred_element_type=jnp.float32)
    sum_one, sum_two = lax.psum(
        (jnp.sum(grad_norm, axis=0), jnp.sum(grad_norm * mixed_hat, axis=0)), "rep"
    )
    grad_mixed = (inv_hidden * (grad_norm - sum_one / H - mixed_hat * (sum_two / H))).astype(
        jnp.bfloat16
    )
    grad_local = jnp.einsum("hij,hjk->hik", grad_mixed, carried, preferred_element_type=jnp.float32)
    swapped = lax.psum_scatter(
        jnp.einsum(
            "hij,hik->jhk", grad_mixed, local_side, preferred_element_type=jnp.float32
        ).astype(jnp.bfloat16),
        "dap",
        scatter_dimension=0,
        tiled=True,
    ).astype(jnp.float32)
    grad_remote = jnp.swapaxes(swapped, 0, 1)
    sigmoid_left = jax.nn.sigmoid(projected[gate_left])
    sigmoid_right = jax.nn.sigmoid(projected[gate_right])
    pieces = [None, None, None, None]
    pieces[value_left] = grad_local * sigmoid_left
    pieces[gate_left] = grad_local * projected[value_left] * sigmoid_left * (1.0 - sigmoid_left)
    pieces[value_right] = grad_remote * sigmoid_right
    pieces[gate_right] = (
        grad_remote * projected[value_right] * sigmoid_right * (1.0 - sigmoid_right)
    )
    grad_proj = jnp.stack(pieces).astype(jnp.bfloat16)
    d_weights = jnp.einsum("rnc,qhrn->qch", normed, grad_proj, preferred_element_type=jnp.float32)
    partial_sum = jnp.einsum(
        "qhrn,qch->rnc", grad_proj, weights, preferred_element_type=jnp.float32
    )
    partial_sum = partial_sum + jnp.einsum(
        "rnd,cd->rnc", grad_gate, gate_w, preferred_element_type=jnp.float32
    )
    grad_normed = lax.psum(partial_sum.astype(jnp.bfloat16), "rep").astype(jnp.float32)
    grad_in = grad_out + pair_inverse * (
        grad_normed
        - jnp.mean(grad_normed, axis=-1, keepdims=True)
        - pair_hat * jnp.mean(grad_normed * pair_hat, axis=-1, keepdims=True)
    )
    return (grad_in, d_weights, d_gate, d_output)


def residue_permutation(chain_index, chain_swap):
    chains = chain_swap.shape[0]
    chain_ids = jnp.arange(chains, dtype=jnp.int32)
    starts = jnp.sum((chain_index[None, :] < chain_ids[:, None]).astype(jnp.int32), axis=1)
    mapped_starts = jnp.sum(
        (chain_swap[:, None] == chain_ids[None, :]).astype(jnp.int32) * starts[None, :], axis=1
    )
    member = (chain_index[:, None] == chain_ids[None, :]).astype(jnp.int32)
    own_start = jnp.sum(member * starts[None, :], axis=1)
    new_start = jnp.sum(member * mapped_starts[None, :], axis=1)
    positions = jnp.arange(chain_index.shape[0], dtype=jnp.int32)
    return positions - own_start + new_start


def per_device(
    pair_input,
    outgoing_weights,
    outgoing_gate,
    outgoing_output,
    incoming_weights,
    incoming_gate,
    incoming_output,
    distogram_head,
    distance_bins,
    chain_index,
    chain_swap,
):
    row_count = pair_input.shape[0]
    residues = pair_input.shape[1]
    middle, stored_out = triangle_forward(
        pair_input, outgoing_weights, outgoing_gate, outgoing_output, (0, 1, 2, 3)
    )
    middle_t = jnp.swapaxes(
        lax.all_to_all(middle, "dap", split_axis=1, concat_axis=0, tiled=True), 0, 1
    )
    final_t, stored_in = triangle_forward(
        middle_t, incoming_weights, incoming_gate, incoming_output, (2, 3, 0, 1)
    )
    final_rows = jnp.swapaxes(
        lax.all_to_all(final_t, "dap", split_axis=1, concat_axis=0, tiled=True), 0, 1
    )
    half_rows = row_count // lax.axis_size("rep")
    rep_index = lax.axis_index("rep")
    own_rows = lax.dynamic_slice_in_dim(final_rows, rep_index * half_rows, half_rows, 0)
    own_cols = lax.dynamic_slice_in_dim(final_t, rep_index * half_rows, half_rows, 0)
    two_views = jnp.stack([own_rows, own_cols])
    view_logits = jnp.einsum(
        "srnc,cb->srnb", two_views, distogram_head, preferred_element_type=jnp.float32
    )
    logits = view_logits[0] + view_logits[1]
    permuted = residue_permutation(chain_index, chain_swap)
    row_ids = (
        lax.axis_index("dap") * row_count
        + rep_index * half_rows
        + jnp.arange(half_rows, dtype=jnp.int32)
    )
    target = jnp.take(
        jnp.take(distance_bins, jnp.take(permuted, row_ids), axis=0), permuted, axis=1
    )
    log_total = jnp.log(jnp.sum(jnp.exp(logits), axis=-1, keepdims=True))
    bins = distogram_head.shape[1]
    onehot = (target[:, :, None] == jnp.arange(bins, dtype=jnp.int32)[None, None, :]).astype(
        jnp.float32
    )
    grad_logits = (jnp.exp(logits - log_total) - onehot).astype(jnp.bfloat16)
    d_head = jnp.einsum("srnc,rnb->cb", two_views, grad_logits, preferred_element_type=jnp.float32)
    grad_half = jnp.einsum(
        "rnb,cb->rnc", grad_logits, distogram_head, preferred_element_type=jnp.float32
    )
    grad_rows = lax.all_gather(grad_half.astype(jnp.bfloat16), "rep", axis=0, tiled=True).astype(
        grad_half.dtype
    )
    mirrored = jnp.swapaxes(
        lax.all_to_all(
            grad_rows.astype(jnp.bfloat16), "dap", split_axis=1, concat_axis=0, tiled=True
        ).astype(grad_rows.dtype),
        0,
        1,
    )
    grad_t = grad_rows + mirrored
    grad_mid_t, dw_in, dg_in, do_in = triangle_backward(
        grad_t, stored_in, incoming_weights, incoming_gate, incoming_output, (2, 3, 0, 1)
    )
    grad_mid = jnp.swapaxes(
        lax.all_to_all(
            grad_mid_t.astype(jnp.bfloat16), "dap", split_axis=1, concat_axis=0, tiled=True
        ).astype(grad_mid_t.dtype),
        0,
        1,
    )
    pair_grad, dw_out, dg_out, do_out = triangle_backward(
        grad_mid, stored_out, outgoing_weights, outgoing_gate, outgoing_output, (0, 1, 2, 3)
    )
    grad_sums = (
        lax.psum(dw_out.astype(jnp.bfloat16), "dap").astype(jnp.float32),
        lax.psum(dg_out.astype(jnp.bfloat16), "dap").astype(jnp.float32),
        lax.psum(do_out.astype(jnp.bfloat16), "dap").astype(jnp.float32),
        lax.psum(dw_in.astype(jnp.bfloat16), "dap").astype(jnp.float32),
        lax.psum(dg_in.astype(jnp.bfloat16), "dap").astype(jnp.float32),
        lax.psum(do_in.astype(jnp.bfloat16), "dap").astype(jnp.float32),
    )
    head_total = lax.psum(d_head, ("dap", "rep"))
    inv_count = 1.0 / residues
    return (
        pair_grad,
        grad_sums[0] * inv_count,
        grad_sums[1] * inv_count,
        grad_sums[2] * inv_count,
        grad_sums[3] * inv_count,
        grad_sums[4] * inv_count,
        grad_sums[5] * inv_count,
        head_total * inv_count,
    )


F32, BF16 = jnp.float32, jnp.bfloat16
CH = 128
LANES = 128
GROUP = 2
UNROLL = 32


def dot(a, b, da=1, db=0):
    return lax.dot_general(a, b, (((da,), (db,)), ((), ())), preferred_element_type=F32)


def sigmoid(v):
    return 0.5 * jnp.tanh(0.5 * v) + 0.5


def mean0(v):
    return jnp.mean(v, axis=0, keepdims=True)


def norm0(v):
    centred = v - mean0(v)
    inverse = lax.rsqrt(mean0(centred * centred) + epsilon)
    return (centred * inverse, inverse)


def rounded(v):
    return v.astype(BF16).astype(F32)


def plane_load(ref, group, half, channels):
    tiles = [
        ref[pl.ds(group * GROUP + t, channels, stride=half), :] for t in range(GROUP)
    ]
    return jnp.concatenate(tiles, axis=1)


def plane_store(ref, group, half, values):
    for t in range(GROUP):
        ref[pl.ds(group * GROUP + t, values.shape[0], stride=half), :] = values[
            :, t * LANES : (t + 1) * LANES
        ]


def matrix_load(ref, channel, half):
    packed = ref[pl.ds(pl.multiple_of(channel * half, half), half), :]
    n = LANES // 2
    return jnp.concatenate([packed[:, :n], packed[:, n:]], axis=0)


def matrix_store(ref, channel, half, values):
    packed = jnp.concatenate([values[:half], values[half:]], axis=1)
    ref[pl.ds(pl.multiple_of(channel * half, half), half), :] = packed


def over(count, body):
    def step(index, carry):
        body(index)
        return carry

    lax.fori_loop(0, count, step, 0)


def over_channels(channels, half, sources, targets, body):
    def step(index):
        channels_here = [index * UNROLL + u for u in range(UNROLL)]
        loaded = [[matrix_load(ref, h, half) for ref in sources] for h in channels_here]
        results = [body(*values) for values in loaded]
        for h, values in zip(channels_here, results):
            for ref, value in zip(targets, values):
                matrix_store(ref, h, half, value)

    over(channels // UNROLL, step)


def part_kernel(
    place,
    pair,
    mats,
    head,
    target,
    pair_grad,
    dw_out,
    dg_out,
    do_out,
    dw_in,
    dg_in,
    do_in,
    d_head,
    down,
    up,
    z0,
    z1,
    z2,
    go,
    p1,
    p2,
    y1,
    y2,
    a1,
    b1,
    x1,
    a2,
    b2,
    x2,
    lg,
    acc1,
    acc2,
    acc_o1,
    acc_o2,
    acc_h,
    target_t,
):
    n = pair.shape[0]
    half = n // 2
    groups = half // GROUP
    own_rows = pair_grad.shape[0]
    width = dg_out.shape[0]
    bins = head.shape[0]
    def square(index):
        return jnp.concatenate([mats[0, index], mats[1, index]], axis=0)

    def turned(values):
        return values.astype(F32).T.astype(BF16)

    for side in range(2):
        for q in range(5):
            matrix = square(side * 6 + q)
            down[side, q * CH : (q + 1) * CH, :] = matrix
            up[side, :, q * CH : (q + 1) * CH] = turned(matrix)
    out_n1, out_n2 = square(5), square(11)
    out_t1, out_t2 = turned(out_n1), turned(out_n2)
    head_t = head[...]
    heads = turned(jnp.concatenate([head_t, head_t], axis=0))
    target_t[...] = target[...].T
    for ref in (acc1, acc2, acc_o1, acc_o2, acc_h):
        ref[...] = jnp.zeros_like(ref)

    def project(g, z, side, proj, a, b):
        hat, _ = norm0(z)
        p = dot(down[side], hat.astype(BF16))
        proj[g] = p
        plane_store(a, g, half, rounded(sigmoid(p[CH : 2 * CH]) * p[:CH]))
        plane_store(b, g, half, rounded(sigmoid(p[3 * CH : 4 * CH]) * p[2 * CH : 3 * CH]))

    def mix_norm(g, x):
        v = plane_load(x, g, half, CH)
        m = mean0(v)
        s = lax.rsqrt(mean0(v * v) - m * m + epsilon)
        return ((v - m) * s, s)

    def update(g, z, x, proj, y, out_t):
        hat, _ = mix_norm(g, x)
        upd = dot(out_t, hat.astype(BF16))
        y[g] = upd
        return rounded(z + sigmoid(proj[g, 4 * CH :, :]) * upd)

    def first(g):
        tiles = []
        for t in range(GROUP):
            row = g * GROUP + t
            cells = jnp.concatenate([pair[row].astype(F32), pair[row + half].astype(F32)], axis=0)
            tiles.append(cells.T)
        z = jnp.concatenate(tiles, axis=1)
        z0[g] = z
        project(g, z, 0, p1, a1, b1)

    over(groups, first)

    def mix_one(left, right):
        return (dot(left.astype(BF16), right.astype(BF16), 1, 1),)

    over_channels(CH, half, (a1, b1), (x1,), mix_one)

    def second(g):
        z = update(g, z0[g], x1, p1, y1, out_t1)
        z1[g] = z
        project(g, z, 1, p2, a2, b2)

    over(groups, second)

    def mix_two(left, right):
        return (dot(left.T.astype(BF16), right.astype(BF16)),)

    over_channels(CH, half, (a2, b2), (x2,), mix_two)

    def third(g):
        z = update(g, z1[g], x2, p2, y2, out_t2).astype(BF16)
        z2[g] = z
        plane_store(lg, g, half, dot(head_t, z))

    over(groups, third)

    def mirror(values):
        return (values + values.T,)

    over_channels(bins, half, (lg,), (lg,), mirror)

    def enter(g, grad, x, proj, y, out_n, acc_o):
        upd = y[g]
        gate = sigmoid(proj[g, 4 * CH :, :])
        scaled = grad * gate
        proj[g, 4 * CH :, :] = scaled * upd * (1.0 - gate)
        gy = scaled.astype(BF16)
        hat, s = mix_norm(g, x)
        acc_o[...] += dot(hat.astype(BF16), gy, 1, 1)
        gxn = dot(out_n, gy)
        gx = s * (gxn - mean0(gxn) - hat * mean0(gxn * hat))
        plane_store(x, g, half, rounded(gx))

    def lane_row(ref, g):
        rows = [g * GROUP + t + upper * half for t in range(GROUP) for upper in range(2)]
        return jnp.concatenate([ref[pl.ds(row, 1), :] for row in rows], axis=1)

    def loss(g):
        logits = plane_load(lg, g, half, bins)
        prob = jnp.exp(logits - jnp.log(jnp.sum(jnp.exp(logits), axis=0, keepdims=True)))
        ids = lax.broadcasted_iota(jnp.int32, logits.shape, 0).astype(F32)
        hot = (ids == lane_row(target, g)).astype(F32)
        hot_t = (ids == lane_row(target_t, g)).astype(F32)
        both = jnp.concatenate([prob - hot, prob - hot_t], axis=0).astype(BF16)
        grad = dot(heads, both)
        go[g] = grad
        acc_h[...] += dot(both, z2[g], 1, 1)
        enter(g, grad, x2, p2, y2, out_n2, acc_o2)

    over(groups, loss)

    def back_two(left, right, grad):
        gx = grad.astype(BF16)
        return (dot(right.astype(BF16), gx, 1, 1), dot(left.astype(BF16), gx))

    over_channels(CH, half, (a2, b2, x2), (a2, b2), back_two)

    def leave(g, z, proj, a, b, side, acc):
        ga = plane_load(a, g, half, CH)
        gb = plane_load(b, g, half, CH)
        sa = sigmoid(proj[g, CH : 2 * CH, :])
        sb = sigmoid(proj[g, 3 * CH : 4 * CH, :])
        ta, tb = ga * sa, gb * sb
        pieces = [
            ta,
            ta * proj[g, :CH, :] * (1.0 - sa),
            tb,
            tb * proj[g, 2 * CH : 3 * CH, :] * (1.0 - sb),
            proj[g, 4 * CH :, :],
        ]
        gp = jnp.concatenate([v.astype(BF16) for v in pieces], axis=0)
        hat, inverse = norm0(z)
        acc[...] += dot(gp, hat.astype(BF16), 1, 1)
        return (gp, hat, inverse)

    def finish(g, side, grad, gp, hat, inverse):
        gn = dot(up[side], gp)
        return grad + inverse * (gn - mean0(gn) - hat * mean0(gn * hat))

    def fourth(g):
        grad = finish(g, 1, go[g], *leave(g, z1[g], p2, a2, b2, 1, acc2))
        go[g] = grad
        enter(g, grad, x1, p1, y1, out_n1, acc_o1)

    over(groups, fourth)

    def back_one(left, right, gx):
        ga = dot(gx.astype(BF16), right.astype(BF16))
        return (ga, dot(gx.T.astype(BF16), left.astype(BF16)))

    over_channels(CH, half, (a1, b1, x1), (a1, b1), back_one)

    row = place[0]
    upper = row // half
    low = row - upper * half
    n_lane = LANES // 2

    def last(g):
        gp, hat, inverse = leave(g, z0[g], p1, a1, b1, 0, acc1)

        @pl.when((g * GROUP >= low) & (g * GROUP < low + own_rows))
        def _():
            grad = finish(g, 0, go[g], gp, hat, inverse)
            for t in range(GROUP):
                cells = grad[:, t * LANES : (t + 1) * LANES].T
                chosen = jnp.where(upper == 0, cells[:n_lane], cells[n_lane:])
                pair_grad[g * GROUP + t - low] = chosen

    over(groups, last)

    scale = 1.0 / n
    start = pl.multiple_of(place[1], width)
    for acc, dw, dg in ((acc1, dw_out, dg_out), (acc2, dw_in, dg_in)):
        for q in range(4):
            dw[q] = acc[pl.ds(q * CH + start, width), :] * scale
        dg[...] = acc[pl.ds(4 * CH + start, width), :] * scale
    do_out[...] = acc_o1[pl.ds(start, width), :] * scale
    do_in[...] = acc_o2[pl.ds(start, width), :] * scale
    d_head[...] = (acc_h[:bins] + acc_h[bins:]) * scale


def gather_kernel(
    dap,
    pair,
    w_out,
    g_out,
    o_out,
    w_in,
    g_in,
    o_in,
    pair_all,
    mats,
    send_sem,
    recv_sem,
    send_mats,
    recv_mats,
):
    fars = dap // 2
    mine, rep = lax.axis_index("dap"), lax.axis_index("rep")
    far, near = mine // 2, mine % 2
    size = pair_all.shape[1]

    def origin(step):
        return lax.rem(far - step + fars, fars)

    def slot(origin_far, origin_near, origin_rep):
        return (origin_far * 2 + origin_near) * 2 + origin_rep

    along = [{"dap": lax.rem(far + step, fars) * 2 + near, "rep": rep} for step in range(fars)]
    across = {"dap": far * 2 + 1 - near, "rep": rep}
    partner = {"dap": mine, "rep": 1 - rep}

    barrier = pltpu.get_barrier_semaphore()
    peers = along[1:] + [across, partner]
    for peer in peers:
        pl.semaphore_signal(barrier, inc=1, device_id=peer, device_id_type=pl.DeviceIdType.MESH)

    own = slot(far, near, rep)
    pair_all[own] = pair[pl.ds(pl.multiple_of(rep * size, size), size), :]
    mats[rep, 0:4] = w_out[...]
    mats[rep, 4] = g_out[...]
    mats[rep, 5] = o_out[...]
    mats[rep, 6:10] = w_in[...]
    mats[rep, 10] = g_in[...]
    mats[rep, 11] = o_in[...]
    pl.semaphore_wait(barrier, len(peers))

    started = []

    def send(place, index, device):
        copy = pltpu.make_async_remote_copy(
            src_ref=pair_all.at[place],
            dst_ref=pair_all.at[place],
            send_sem=send_sem.at[index],
            recv_sem=recv_sem.at[index],
            device_id=device,
            device_id_type=pl.DeviceIdType.MESH,
        )
        copy.start()
        started.append(copy)

    def await_block(place, index, device):
        pltpu.make_async_remote_copy(
            src_ref=pair_all.at[place],
            dst_ref=pair_all.at[place],
            send_sem=send_sem.at[index],
            recv_sem=recv_sem.at[index],
            device_id=device,
            device_id_type=pl.DeviceIdType.MESH,
        ).wait_recv()

    near_base = fars
    rep_base = 2 * fars
    for step in range(1, fars):
        send(own, step, along[step])
    send(own, near_base, across)
    copy_mats = pltpu.make_async_remote_copy(
        src_ref=mats.at[rep],
        dst_ref=mats.at[rep],
        send_sem=send_mats,
        recv_sem=recv_mats,
        device_id=partner,
        device_id_type=pl.DeviceIdType.MESH,
    )
    copy_mats.start()
    send(own, rep_base, partner)
    for step in range(1, fars):
        place = slot(origin(step), near, rep)
        await_block(place, step, along[step])
        send(place, near_base + step, across)
        send(place, rep_base + step, partner)
    for step in range(fars):
        place = slot(origin(step), 1 - near, rep)
        await_block(place, near_base + step, across)
        send(place, rep_base + fars + step, partner)
    for step in range(fars):
        await_block(slot(origin(step), near, 1 - rep), rep_base + step, partner)
        await_block(slot(origin(step), 1 - near, 1 - rep), rep_base + fars + step, partner)
    copy_mats.wait_recv()
    for copy in started:
        copy.wait_send()
    copy_mats.wait_send()


def gather_part(dap, pair, *matrices):
    size = pair.shape[0] // 2
    width = matrices[2].shape[0]
    fars = dap // 2
    vmem = pl.BlockSpec(memory_space=pltpu.VMEM)
    return pl.pallas_call(
        functools.partial(gather_kernel, dap),
        out_shape=(
            jax.ShapeDtypeStruct((dap * 2, size, CH), BF16),
            jax.ShapeDtypeStruct((2, 12, width, CH), BF16),
        ),
        in_specs=[vmem] * 7,
        out_specs=(vmem, vmem),
        scratch_shapes=[
            pltpu.SemaphoreType.DMA((4 * fars,)),
            pltpu.SemaphoreType.DMA((4 * fars,)),
            pltpu.SemaphoreType.DMA,
            pltpu.SemaphoreType.DMA,
        ],
        compiler_params=pltpu.CompilerParams(
            collective_id=0, has_side_effects=True, vmem_limit_bytes=32 * 1024 * 1024
        ),
    )(pair, *matrices)


def whole_part(dap, rep):
    def run(
        pair_input,
        outgoing_weights,
        outgoing_gate,
        outgoing_output,
        incoming_weights,
        incoming_gate,
        incoming_output,
        distogram_head,
        distance_bins,
        chain_index,
        chain_swap,
    ):
        rows, n, _ = pair_input.shape
        bins = distogram_head.shape[1]
        width = outgoing_weights.shape[2]
        pair_all, mats = gather_part(
            dap,
            pair_input.reshape(rows * n, CH),
            jnp.swapaxes(outgoing_weights, 1, 2),
            outgoing_gate.T,
            outgoing_output,
            jnp.swapaxes(incoming_weights, 1, 2),
            incoming_gate.T,
            incoming_output,
        )
        permuted = residue_permutation(chain_index, chain_swap)
        positions = jnp.arange(n, dtype=jnp.int32)
        mover = (permuted[:, None] == positions[None, :]).astype(BF16)
        moved = jnp.einsum(
            "ia,ab,jb->ij", mover, distance_bins.astype(BF16), mover, preferred_element_type=F32
        )
        groups = n // 2 // GROUP

        place = jnp.stack([lax.axis_index("dap") * rows, lax.axis_index("rep") * width])
        shape = jax.ShapeDtypeStruct
        vmem = pl.BlockSpec(memory_space=pltpu.VMEM)
        block = GROUP * LANES
        cells = pltpu.VMEM((groups, CH, block), F32)
        plane = pltpu.VMEM((CH * n // 2, LANES), F32)
        projected = pltpu.VMEM((groups, 5 * CH, block), F32)
        square = pltpu.VMEM((CH, CH), F32)
        outs = pl.pallas_call(
            part_kernel,
            out_shape=(
                shape((rows, n, CH), F32),
                shape((4, width, CH), F32),
                shape((width, CH), F32),
                shape((width, CH), F32),
                shape((4, width, CH), F32),
                shape((width, CH), F32),
                shape((width, CH), F32),
                shape((bins, CH), F32),
            ),
            in_specs=[pl.BlockSpec(memory_space=pltpu.SMEM)] + [vmem] * 4,
            out_specs=tuple([vmem] * 8),
            scratch_shapes=[
                pltpu.VMEM((2, 5 * CH, CH), BF16),
                pltpu.VMEM((2, CH, 5 * CH), BF16),
                cells,
                cells,
                pltpu.VMEM((groups, CH, block), BF16),
                cells,
                projected,
                projected,
                cells,
                cells,
                plane,
                plane,
                plane,
                plane,
                plane,
                plane,
                pltpu.VMEM((bins * n // 2, LANES), F32),
                pltpu.VMEM((5 * CH, CH), F32),
                pltpu.VMEM((5 * CH, CH), F32),
                square,
                square,
                square,
                pltpu.VMEM((n, n), F32),
            ],
            compiler_params=pltpu.CompilerParams(vmem_limit_bytes=60 * 1024 * 1024),
        )(
            place.astype(jnp.int32),
            pair_all.reshape(dap * rows, n, CH),
            mats,
            distogram_head.T,
            moved,
        )
        pair_grad, dw_out, dg_out, do_out, dw_in, dg_in, do_in, d_head = outs
        return (
            pair_grad,
            jnp.swapaxes(dw_out, 1, 2),
            dg_out.T,
            do_out,
            jnp.swapaxes(dw_in, 1, 2),
            dg_in.T,
            do_in,
            d_head.T,
        )

    return run


def solution(mesh):
    dap, rep = mesh.shape["dap"], mesh.shape["rep"]

    def plan(*arrays):
        residues, channels = arrays[0].shape[1], arrays[0].shape[2]
        width, bins = arrays[1].shape[2], arrays[7].shape[1]
        rows = arrays[0].shape[0]
        small = residues == LANES // 2 and channels == CH and width * rep == CH
        small = small and bins * 2 == CH and rep == 2 and dap % 2 == 0 and rows % 2 == 0 and rows % GROUP == 0
        small = small and (residues // 2) % rows == 0
        return (whole_part(dap, rep) if small else per_device)(*arrays)

    return jax.shard_map(
        plan,
        mesh=mesh,
        in_specs=(
            P(("groups", "dap"), None, None),
            P(None, None, "rep"),
            P(None, "rep"),
            P("rep", None),
            P(None, None, "rep"),
            P(None, "rep"),
            P("rep", None),
            P(),
            P("groups", None),
            P("groups"),
            P("groups"),
        ),
        out_specs=(
            P(("groups", "dap"), None, None),
            P("groups", None, "rep"),
            P("groups", "rep"),
            P(("groups", "rep"), None),
            P("groups", None, "rep"),
            P("groups", "rep"),
            P(("groups", "rep"), None),
            P("groups", None),
        ),
        check_vma=False,
    )
```
